768 devices in a mesh: row: 96 (over x, y, z_lo), feat: 8 (over z_hi, core).
Axes of the slice: x: 4, y: 8, z: 12 (z_hi: 4, z_lo: 3; z = z_hi * 3 + z_lo), core: 2. Of those that a mesh axis runs over, the one named last changes fastest.
Arguments:
- features: bfloat16 [24576, 128], P('row', 'feat'), may hold values from -6 to 6
- weight: bfloat16 [128, 256], P('feat'), may hold values from -0.5 to 0.5
- norm_scale: float32 [24576], P('row'), may hold values from 0.3 to 3
- tile_rows: int32 [4608], P('row'), may hold values from 0 to 1
- tile_cols: int32 [4608], P('row'), may hold values from 0 to 191
- tile_vals: bfloat16 [4608, 128, 128], P('row'), may hold values from -0.109375 to 0.109375
- cotangent: bfloat16 [24576, 256], P('row', 'feat'), may hold values from -6 to 6
Outputs:
- activated: bfloat16 [24576, 256], P('row', 'feat')
- weight_grad: float32 [128, 256], P('feat')
- feature_grad: bfloat16 [24576, 128], P('row', 'feat')
The draws below stay inside these ranges and needn't reach their ends.
Inputs may be any that keep to these rules, and one draw needn't show every extreme that they name: `tile_cols`: tiles may repeat a coordinate; repeated tiles add.
All inputs are finite; a program needn't handle non-finite values.
Results may differ from the reference program's by a relative error of at most 0.0068.
Values may be sent and summed in bfloat16 or wider, within the bound.
No kernel may reach another device: no remote copies, remote signals or barrier semaphores. Data moves between devices by JAX's collectives and lax.ppermute only.
A program may use at most 64 MiB of HBM per device.

```python
import math
import jax
import jax.numpy as jnp
import numpy as np
from jax import lax

F = 128
H = 256
TILE = 128
ROWS_DEV = 256
TILES = 48
NODES = 24576
ROW_TILES = 2
COL_TILES = 192
TILES_ALL = 4608
N_ROW = 96


def set_ends(values, own_key, low, high):
    longest = values.shape.index(max(values.shape))
    spots = []
    for shift in (0, 1):
        where = [jax.random.randint(jax.random.fold_in(own_key, axis), (), 0, length) for axis, length in enumerate(values.shape)]
        where[longest] = (where[longest] + shift) % values.shape[longest]
        spots.append(tuple(where))
    return values.at[spots[0]].set(low).at[spots[1]].set(high)


def level_of(own_key, dims, cuts, least, largest):
    loudness, own = 1.0, jax.random.fold_in(own_key, 6)
    for dim, blocks in cuts:
        steps = jnp.exp(jax.random.uniform(jax.random.fold_in(own, dim), (blocks,), jnp.float32, least / len(cuts), largest / len(cuts)))
        loudness = loudness * jnp.repeat(steps, dims[dim] // blocks).reshape([-1 if axis == dim else 1 for axis in range(len(dims))])
    return loudness


def cumulative_ranks(count, lean):
    loads = [(1 << 20) // math.isqrt(rank ** lean) + 1 for rank in range(1, count + 1)]
    scale = 1 + sum(loads) // (1 << 30)
    return np.cumsum(np.array([max(1, weight // scale) for weight in loads]))


def skewed_ids(own_key, extent, amount, skew):
    grid = cumulative_ranks(amount, skew)
    pick = jax.random.randint(jax.random.fold_in(own_key, 1), extent, 0, int(grid[amount - 1]))
    grade = jnp.searchsorted(jnp.asarray(grid, jnp.int32), pick, side="right")
    return jax.random.permutation(jax.random.fold_in(own_key, 2), amount)[grade].astype(jnp.int32)


def bell_draw(own_key, dims, deviation, most, shards=(), kind=jnp.bfloat16):
    loudness = level_of(own_key, dims, shards, -0.22, 0.18) if shards else 1.0
    drawn = jax.random.normal(own_key, dims, jnp.float32) * deviation * loudness
    return jnp.minimum(jnp.maximum(drawn, -most), most).astype(kind)


def setup_inputs(seed: int = 0) -> dict:
    seeds = jax.random.split(jax.random.key(seed), 8)
    return {
        "features": bell_draw(seeds[0], (NODES, F), 1.0, 6.0, ((0, 96), (1, 8))),
        "weight": bell_draw(seeds[1], (F, H), F ** -0.5, 0.5, ((0, 8),)),
        "norm_scale": jnp.clip(jnp.exp(math.log(3.0) - 2.3025851 * jax.random.uniform(seeds[2], (NODES,), jnp.float32) ** level_of(seeds[2], (NODES,), ((0, 96),), -0.2, 0.2)), 0.3, 3.0),
        "tile_rows": set_ends(jax.random.randint(seeds[3], (TILES_ALL,), 0, ROW_TILES), jax.random.fold_in(seeds[3], 1), 0, ROW_TILES - 1).astype(jnp.int32),
        "tile_cols": set_ends(skewed_ids(seeds[4], (TILES_ALL,), COL_TILES, 2), jax.random.fold_in(seeds[4], 3), 0, COL_TILES - 1).astype(jnp.int32),
        "tile_vals": bell_draw(seeds[5], (TILES_ALL, TILE, TILE), (TILE * TILES // ROW_TILES) ** -0.5, 0.109375, ((0, 96),)),
        "cotangent": bell_draw(seeds[6], (NODES, H), 1.0, 6.0, ((0, 96), (1, 8))),
    }


def reference(features, weight, norm_scale, tile_rows, tile_cols, tile_vals, cotangent):
    row_tiles = ROWS_DEV // TILE
    col_tiles = NODES // TILE
    highest = lax.Precision.HIGHEST
    scaled = norm_scale[:, None]
    projected = jnp.dot(features, weight, preferred_element_type=jnp.float32)
    source = (projected * scaled).astype(jnp.bfloat16)
    source_tiles = source.reshape(col_tiles, TILE, H)
    dev_vals = tile_vals.reshape(N_ROW, TILES, TILE, TILE)
    dev_rows = tile_rows.reshape(N_ROW, TILES).astype(jnp.int32)
    dev_cols = tile_cols.reshape(N_ROW, TILES).astype(jnp.int32)
    select_base = jnp.arange(row_tiles, dtype=jnp.int32)

    def forward_one(packed):
        block_vals, block_rows, block_cols = packed
        picked = source_tiles[block_cols].astype(jnp.float32)
        contrib = jnp.einsum("tij,tjh->tih", block_vals.astype(jnp.float32), picked, precision=highest)
        select = (block_rows[None, :] == select_base[:, None]).astype(jnp.float32)
        return jnp.einsum("rt,tih->rih", select, contrib, precision=highest)

    summed = lax.map(forward_one, (dev_vals, dev_rows, dev_cols)).reshape(NODES, H)
    pre_act = summed * scaled
    activated = jax.nn.silu(pre_act).astype(jnp.bfloat16)
    sigma = jax.nn.sigmoid(pre_act)
    slope = sigma * (1.0 + pre_act * (1.0 - sigma))
    back_in = (cotangent.astype(jnp.float32) * slope * scaled).astype(jnp.bfloat16)
    back_dev = back_in.reshape(N_ROW, row_tiles, TILE, H)

    def backward_step(total, packed):
        block_vals, block_rows, block_cols, block_back = packed
        terms = jnp.einsum("tji,tjh->tih", block_vals.astype(jnp.float32),
                           block_back[block_rows].astype(jnp.float32), precision=highest)
        return total.at[block_cols].add(terms), None

    start_total = jnp.zeros((col_tiles, TILE, H), jnp.float32)
    grad_source, _ = lax.scan(backward_step, start_total, (dev_vals, dev_rows, dev_cols, back_dev))
    grad_proj = (grad_source.reshape(NODES, H) * scaled).astype(jnp.bfloat16)
    weight_grad = lax.dot_general(features, grad_proj, (((0,), (0,)), ((), ())),
                                  preferred_element_type=jnp.float32)
    feature_grad = lax.dot_general(grad_proj, weight, (((1,), (1,)), ((), ())),
                                   preferred_element_type=jnp.float32).astype(jnp.bfloat16)
    return activated, weight_grad, feature_grad
```

```python
import jax
import jax.numpy as jnp
from jax import lax
from jax.experimental import pallas as pl
from jax.experimental.pallas import tpu as pltpu
from jax.sharding import PartitionSpec as P

F32 = jnp.float32
BF16 = jnp.bfloat16
NT = (((1,), (1,)), ((), ()))
NN = (((1,), (0,)), ((), ()))


def halves(value):
    head = value.astype(BF16)
    return head, (value - head.astype(F32)).astype(BF16)


def forward_kernel(rows_ref, cols_ref, tiles_ref, nodes_ref, sum_ref):
    row_tiles = sum_ref.shape[0]
    totals = [jnp.zeros(sum_ref.shape[1:], F32) for _ in range(row_tiles)]
    for t in range(tiles_ref.shape[0]):
        term = lax.dot_general(
            nodes_ref[cols_ref[t]], tiles_ref[t], NT, preferred_element_type=F32
        )
        for i in range(row_tiles):
            totals[i] = totals[i] + jnp.where(rows_ref[t] == i, term, 0.0)
    for i in range(row_tiles):
        sum_ref[i] = totals[i]


def backward_kernel(rows_ref, cols_ref, tiles_ref, back_ref, out_ref, total_ref):
    total_ref[...] = jnp.zeros_like(total_ref)
    for t in range(tiles_ref.shape[0]):
        total_ref[cols_ref[t]] += lax.dot_general(
            back_ref[rows_ref[t]], tiles_ref[t], NN, preferred_element_type=F32
        )
    out_ref[...] = total_ref[...].astype(out_ref.dtype)


def per_device(features, weight, norm_scale, tile_rows, tile_cols, tile_vals, cotangent):
    rows_dev, feat_part = features.shape
    tile_len = tile_vals.shape[1]
    row_tiles = rows_dev // tile_len
    hid_part = cotangent.shape[1]
    n_row = lax.axis_size("row")
    n_feat = lax.axis_size("feat")
    hidden = hid_part * n_feat
    me = lax.axis_index("feat")
    smem = pl.BlockSpec(memory_space=pltpu.SMEM)
    vmem = pl.BlockSpec(memory_space=pltpu.VMEM)

    def by_tile(value):
        return value.reshape(-1, row_tiles, tile_len).transpose(1, 0, 2)

    def by_row(value):
        return value.transpose(1, 0, 2).reshape(-1, rows_dev)

    scaled = by_tile((features.T.astype(F32) * norm_scale[None, :]).astype(BF16))
    nodes = lax.all_to_all(
        jnp.broadcast_to(scaled[None], (n_row,) + scaled.shape), "row", 0, 0
    ).reshape(n_row * row_tiles, feat_part, tile_len)
    mixed = pl.pallas_call(
        forward_kernel,
        out_shape=jax.ShapeDtypeStruct((row_tiles, feat_part, tile_len), F32),
        in_specs=[smem, smem, vmem, vmem],
        out_specs=vmem,
        compiler_params=pltpu.CompilerParams(vmem_limit_bytes=16 * 2**20),
    )(tile_rows, tile_cols, tile_vals, nodes)
    mixed = by_row(mixed)

    head, rest = halves(mixed)
    block = jnp.concatenate([head, rest, weight, cotangent.T], axis=0)
    group = lax.all_to_all(
        jnp.broadcast_to(block[None], (n_feat,) + block.shape), "feat", 0, 0
    )
    cuts = [feat_part, 2 * feat_part, 3 * feat_part]
    all_head, all_rest, all_weight, all_cot = jnp.split(group, cuts, axis=1)
    all_head = all_head.reshape(-1, rows_dev)
    all_rest = all_rest.reshape(-1, rows_dev)
    all_weight = all_weight.reshape(-1, hidden)
    all_cot = all_cot.reshape(hidden, rows_dev)

    tn = (((0,), (0,)), ((), ()))
    pre_act = (
        lax.dot_general(all_weight, all_head, tn, preferred_element_type=F32)
        + lax.dot_general(all_weight, all_rest, tn, preferred_element_type=F32)
    ) * norm_scale[None, :]
    sigma = jax.nn.sigmoid(pre_act)
    slope = sigma * (1.0 + pre_act * (1.0 - sigma))
    back_in = (all_cot.astype(F32) * slope * norm_scale[None, :]).astype(BF16)
    own = lax.dynamic_slice_in_dim(pre_act, me * hid_part, hid_part, 0)
    activated = jax.nn.silu(own).astype(BF16).T

    back = lax.dot_general(weight, back_in, NN, preferred_element_type=F32)
    col_terms = pl.pallas_call(
        backward_kernel,
        out_shape=jax.ShapeDtypeStruct((n_row * row_tiles, feat_part, tile_len), BF16),
        in_specs=[smem, smem, vmem, vmem],
        out_specs=vmem,
        scratch_shapes=[pltpu.VMEM((n_row * row_tiles, feat_part, tile_len), F32)],
        compiler_params=pltpu.CompilerParams(vmem_limit_bytes=16 * 2**20),
    )(tile_rows, tile_cols, tile_vals, by_tile(back.astype(BF16)))

    weight_part = (
        lax.dot_general(head, back_in, NT, preferred_element_type=F32)
        + lax.dot_general(rest, back_in, NT, preferred_element_type=F32)
    ).astype(BF16)
    sent = jnp.concatenate(
        [
            col_terms.reshape(n_row, row_tiles * feat_part, tile_len),
            jnp.broadcast_to(
                weight_part.reshape(1, -1, tile_len),
                (n_row, feat_part * hidden // tile_len, tile_len),
            ),
        ],
        axis=1,
    )
    got = lax.all_to_all(sent, "row", 0, 0)
    total = jnp.sum(got.astype(F32), axis=0)
    grad = by_row(total[: row_tiles * feat_part].reshape(row_tiles, feat_part, tile_len))
    weight_grad = total[row_tiles * feat_part :].reshape(feat_part, hidden)
    feature_grad = (grad * norm_scale[None, :]).astype(BF16).T
    return (activated, weight_grad, feature_grad)


def solution(mesh):
    placed = (
        P("row", "feat"),
        P("feat", None),
        P("row"),
        P("row"),
        P("row"),
        P("row", None, None),
        P("row", "feat"),
    )
    return jax.shard_map(
        per_device,
        mesh=mesh,
        in_specs=placed,
        out_specs=(P("row", "feat"), P("feat", None), P("row", "feat")),
        check_vma=False,
    )
```

```python
import functools

import jax
import jax.numpy as jnp
from jax import lax
from jax.experimental import pallas as pl
from jax.experimental.pallas import tpu as pltpu
from jax.sharding import Mesh, PartitionSpec as P

F32 = jnp.float32
BF16 = jnp.bfloat16
NT = (((1,), (1,)), ((), ()))
NN = (((1,), (0,)), ((), ()))
TN = (((0,), (0,)), ((), ()))
LANES = 128


def halves(value):
    head = value.astype(BF16)
    return head, (value - head.astype(F32)).astype(BF16)


def dot(left, right, dims):
    return lax.dot_general(left, right, dims, preferred_element_type=F32)


def start_kernel(features_ref, norm_ref, out_ref):
    scaled = (features_ref[...].astype(F32) * norm_ref[...]).astype(BF16)
    for n in range(out_ref.shape[0]):
        for i in range(out_ref.shape[1]):
            out_ref[n, i] = scaled[:, i * LANES : (i + 1) * LANES]


def forward_kernel(rows_ref, cols_ref, tiles_ref, nodes_ref, weight_ref, cot_ref, out_ref):
    part = weight_ref.shape[0]
    row_tiles = cot_ref.shape[1] // LANES
    totals = [jnp.zeros((part, LANES), F32) for _ in range(row_tiles)]
    for t in range(tiles_ref.shape[0]):
        term = dot(nodes_ref[cols_ref[t]], tiles_ref[t], NT)
        for i in range(row_tiles):
            totals[i] = totals[i] + jnp.where(rows_ref[t] == i, term, 0.0)
    for i in range(row_tiles):
        head, rest = halves(totals[i])
        cut = slice(i * LANES, (i + 1) * LANES)
        for n in range(out_ref.shape[0]):
            out_ref[n, 0:part, cut] = head
            out_ref[n, part : 2 * part, cut] = rest
    for n in range(out_ref.shape[0]):
        out_ref[n, 2 * part : 3 * part] = weight_ref[...]
        out_ref[n, 3 * part :] = cot_ref[...]


def middle_kernel(
    rows_ref, cols_ref, me_ref, tiles_ref, group_ref, weight_ref, norm_ref, act_ref, out_ref, pre_ref, total_ref
):
    part = weight_ref.shape[0]
    hid_part = act_ref.shape[0]
    n_feat = group_ref.shape[0]
    group = group_ref[...]
    head = group[:, 0:part].reshape(n_feat * part, -1)
    rest = group[:, part : 2 * part].reshape(n_feat * part, -1)
    weight_all = group[:, 2 * part : 3 * part].reshape(n_feat * part, -1)
    cot = group[:, 3 * part :].reshape(n_feat * hid_part, -1)
    norm = norm_ref[...]
    pre = (dot(weight_all, head, TN) + dot(weight_all, rest, TN)) * norm
    pre_ref[...] = pre
    sigma = 1.0 / (1.0 + jnp.exp(-pre))
    slope = sigma * (1.0 + pre * (1.0 - sigma))
    back_in = (cot.astype(F32) * slope * norm).astype(BF16)
    own = pre_ref[pl.ds(pl.multiple_of(me_ref[0] * hid_part, hid_part), hid_part)]
    act_ref[...] = (own / (1.0 + jnp.exp(-own))).astype(BF16)

    back = dot(weight_ref[...], back_in, NN)
    row_tiles = back.shape[1] // LANES
    back_head, back_rest = halves(back)
    back_tiles = [
        jnp.concatenate([h[:, i * LANES : (i + 1) * LANES] for h in (back_head, back_rest)], axis=0)
        for i in range(row_tiles)
    ]
    total_ref[...] = jnp.zeros_like(total_ref)
    for t in range(tiles_ref.shape[0]):
        left = back_tiles[0]
        for i in range(1, row_tiles):
            left = jnp.where(rows_ref[t] == i, back_tiles[i], left)
        both = dot(left, tiles_ref[t], NN)
        total_ref[cols_ref[t]] += both[:part] + both[part:]

    own_head = group_ref[pl.ds(me_ref[0], 1), 0:part][0]
    own_rest = group_ref[pl.ds(me_ref[0], 1), part : 2 * part][0]
    weight_part = dot(own_head, back_in, NT) + dot(own_rest, back_in, NT)
    n_first, n_rows, _ = out_ref.shape
    cols = total_ref.shape[0] // n_first
    total = total_ref[...].astype(BF16).reshape(n_first, cols * part, LANES)
    out_ref[:, : cols * part] = total
    sent = halves(weight_part)
    spot = cols * part
    for value in sent:
        for j in range(value.shape[1] // LANES):
            piece = value[:, j * LANES : (j + 1) * LANES]
            for n in range(n_first):
                out_ref[n, spot : spot + part] = piece
            spot += part


def relay_kernel(got_ref, out_ref, *, own):
    n_peer = out_ref.shape[0]
    total = got_ref[0].astype(F32)
    for n in range(1, got_ref.shape[0]):
        total = total + got_ref[n].astype(F32)
    out_ref[:, :own] = total[: n_peer * own].astype(BF16).reshape(n_peer, own, LANES)
    value = total[n_peer * own :]
    half = value.shape[0] // 2
    head, rest = halves(value[:half] + value[half:])
    for n in range(n_peer):
        out_ref[n, own : own + half] = head
        out_ref[n, own + half :] = rest


def end_kernel(got_ref, norm_ref, grad_ref, weight_ref):
    total = got_ref[0].astype(F32)
    for n in range(1, got_ref.shape[0]):
        total = total + got_ref[n].astype(F32)
    part = grad_ref.shape[0]
    spot = 0
    for i in range(grad_ref.shape[1] // LANES):
        cut = slice(i * LANES, (i + 1) * LANES)
        grad_ref[:, cut] = (total[spot : spot + part] * norm_ref[:, cut]).astype(BF16)
        spot += part
    half = (total.shape[0] - spot) // 2
    for j in range(weight_ref.shape[1] // LANES):
        weight_ref[:, j * LANES : (j + 1) * LANES] = (
            total[spot : spot + part] + total[spot + half : spot + half + part]
        )
        spot += part


SMEM = pl.BlockSpec(memory_space=pltpu.SMEM)
VMEM = pl.BlockSpec(memory_space=pltpu.VMEM)
SCOPED = pltpu.CompilerParams(vmem_limit_bytes=24 * 2**20)


def call(kernel, outs, in_specs, *args, scratch=()):
    return pl.pallas_call(
        kernel,
        out_shape=outs,
        in_specs=in_specs,
        out_specs=jax.tree.map(lambda _: VMEM, outs),
        scratch_shapes=list(scratch),
        compiler_params=SCOPED,
    )(*args)


def per_device(features, weight, norm_scale, tile_rows, tile_cols, tile_vals, cotangent):
    rows_dev, part = features.shape
    tile_len = tile_vals.shape[1]
    row_tiles = rows_dev // tile_len
    hid_part = cotangent.shape[1]
    hidden = weight.shape[1]
    n_first = lax.axis_size(FIRST)
    n_second = lax.axis_size(SECOND)
    n_feat = lax.axis_size(FEAT)
    col_tiles = n_first * n_second * row_tiles
    norm = norm_scale.reshape(1, rows_dev)
    n_z = lax.axis_size("z")
    tile, owner = tile_cols % row_tiles, tile_cols // row_tiles
    owner_z, owner_y = owner % n_z, owner // n_z % n_second
    owner_x = owner // (n_z * n_second)
    spots = ((owner_x * n_z + owner_z) * n_second + owner_y) * row_tiles + tile
    me = lax.axis_index(FEAT).reshape(1).astype(jnp.int32)
    shape = jax.ShapeDtypeStruct

    block = call(
        start_kernel,
        shape((n_second, row_tiles, part, tile_len), BF16),
        [VMEM, VMEM],
        features.T,
        norm,
    )
    block = lax.all_to_all(block, SECOND, 0, 0)
    block = lax.all_to_all(
        jnp.broadcast_to(block[None], (n_first,) + block.shape), FIRST, 0, 0
    )
    group = call(
        forward_kernel,
        shape((n_feat, 3 * part + hid_part, rows_dev), BF16),
        [SMEM, SMEM, VMEM, VMEM, VMEM, VMEM],
        tile_rows,
        spots,
        tile_vals,
        block.reshape(col_tiles, part, tile_len),
        weight,
        cotangent.T,
    )
    group = lax.all_to_all(group, FEAT, 0, 0)
    own = row_tiles * part
    weight_rows = 2 * part * hidden // tile_len
    activated, sent = call(
        middle_kernel,
        (
            shape((hid_part, rows_dev), BF16),
            shape((n_first, n_second * own + weight_rows, tile_len), BF16),
        ),
        [SMEM, SMEM, SMEM, VMEM, VMEM, VMEM, VMEM],
        tile_rows,
        spots,
        me,
        tile_vals,
        group,
        weight,
        norm,
        scratch=(
            pltpu.VMEM((hidden, rows_dev), F32),
            pltpu.VMEM((col_tiles, part, tile_len), F32),
        ),
    )
    got = lax.all_to_all(sent, FIRST, 0, 0)
    sent = call(
        functools.partial(relay_kernel, own=own),
        shape((n_second, own + weight_rows, tile_len), BF16),
        [VMEM],
        got,
    )
    got = lax.all_to_all(sent, SECOND, 0, 0)
    feature_grad, weight_grad = call(
        end_kernel,
        (shape((part, rows_dev), BF16), shape((part, hidden), F32)),
        [VMEM, VMEM],
        got,
        norm,
    )
    return (activated.T, weight_grad, feature_grad.T)


FIRST, SECOND, FEAT = ("x", "z"), "y", "feat"


def axes_of(rows):
    return (4, 8, 3) if rows == 96 else (2, rows // 4, 2)


def solution(mesh):
    fine = Mesh(
        mesh.devices.reshape(axes_of(mesh.shape["row"]) + (mesh.shape["feat"],)), ("x", "y", "z", "feat")
    )
    row = ("x", "y", "z")
    placed = (
        P(row, "feat"),
        P("feat", None),
        P(row),
        P(row),
        P(row),
        P(row, None, None),
        P(row, "feat"),
    )
    return jax.shard_map(
        per_device,
        mesh=fine,
        in_specs=placed,
        out_specs=(P(row, "feat"), P("feat", None), P(row, "feat")),
        check_vma=False,
    )
```

```python
import functools

import jax
import jax.numpy as jnp
from jax import lax
from jax.experimental import pallas as pl
from jax.experimental.pallas import tpu as pltpu
from jax.sharding import Mesh, PartitionSpec as P

F32 = jnp.float32
BF16 = jnp.bfloat16
NT = (((1,), (1,)), ((), ()))
NN = (((1,), (0,)), ((), ()))
TN = (((0,), (0,)), ((), ()))
LANES = 128


def halves(value):
    head = value.astype(BF16)
    return head, (value - head.astype(F32)).astype(BF16)


def dot(left, right, dims):
    return lax.dot_general(left, right, dims, preferred_element_type=F32)


def start_kernel(features_ref, norm_ref, out_ref):
    scaled = (features_ref[...].astype(F32) * norm_ref[...]).astype(BF16)
    for n in range(out_ref.shape[0]):
        for i in range(out_ref.shape[1]):
            out_ref[n, i] = scaled[:, i * LANES : (i + 1) * LANES]


def spot_of(tile, row_tiles):
    n_z, n_y = lax.axis_size("z"), lax.axis_size("y")
    within, owner = lax.rem(tile, row_tiles), lax.div(tile, row_tiles)
    z, owner = lax.rem(owner, n_z), lax.div(owner, n_z)
    y, x = lax.rem(owner, n_y), lax.div(owner, n_y)
    return ((x * n_z + z) * n_y + y) * row_tiles + within


def forward_kernel(rows_ref, cols_ref, tiles_ref, nodes_ref, weight_ref, cot_ref, out_ref):
    part = weight_ref.shape[0]
    row_tiles = cot_ref.shape[1] // LANES
    totals = [jnp.zeros((part, LANES), F32) for _ in range(row_tiles)]
    for t in range(tiles_ref.shape[0]):
        term = dot(nodes_ref[spot_of(cols_ref[t], row_tiles)], tiles_ref[t], NT)
        for i in range(row_tiles):
            totals[i] = totals[i] + jnp.where(rows_ref[t] == i, term, 0.0)
    for i in range(row_tiles):
        head, rest = halves(totals[i])
        cut = slice(i * LANES, (i + 1) * LANES)
        for n in range(out_ref.shape[0]):
            out_ref[n, 0:part, cut] = head
            out_ref[n, part : 2 * part, cut] = rest
    for n in range(out_ref.shape[0]):
        out_ref[n, 2 * part : 3 * part] = weight_ref[...]
        out_ref[n, 3 * part :] = cot_ref[...]


def middle_kernel(
    rows_ref, cols_ref, tiles_ref, group_ref, weight_ref, norm_ref, act_ref, out_ref, pre_ref, total_ref
):
    me = lax.axis_index(FEAT)
    part = weight_ref.shape[0]
    hid_part = act_ref.shape[0]
    n_feat = group_ref.shape[0]
    group = group_ref[...]
    head = group[:, 0:part].reshape(n_feat * part, -1)
    rest = group[:, part : 2 * part].reshape(n_feat * part, -1)
    weight_all = group[:, 2 * part : 3 * part].reshape(n_feat * part, -1)
    cot = group[:, 3 * part :].reshape(n_feat * hid_part, -1)
    norm = norm_ref[...]
    pre = (dot(weight_all, head, TN) + dot(weight_all, rest, TN)) * norm
    pre_ref[...] = pre
    sigma = 1.0 / (1.0 + jnp.exp(-pre))
    slope = sigma * (1.0 + pre * (1.0 - sigma))
    back_in = (cot.astype(F32) * slope * norm).astype(BF16)
    own = pre_ref[pl.ds(pl.multiple_of(me * hid_part, hid_part), hid_part)]
    act_ref[...] = (own / (1.0 + jnp.exp(-own))).astype(BF16)

    back = dot(weight_ref[...], back_in, NN)
    row_tiles = back.shape[1] // LANES
    back_head, back_rest = halves(back)
    back_tiles = [
        jnp.concatenate([h[:, i * LANES : (i + 1) * LANES] for h in (back_head, back_rest)], axis=0)
        for i in range(row_tiles)
    ]
    total_ref[...] = jnp.zeros_like(total_ref)
    for t in range(tiles_ref.shape[0]):
        left = back_tiles[0]
        for i in range(1, row_tiles):
            left = jnp.where(rows_ref[t] == i, back_tiles[i], left)
        both = dot(left, tiles_ref[t], NN)
        total_ref[spot_of(cols_ref[t], row_tiles)] += both[:part] + both[part:]

    own_head = group_ref[pl.ds(me, 1), 0:part][0]
    own_rest = group_ref[pl.ds(me, 1), part : 2 * part][0]
    weight_part = dot(own_head, back_in, NT) + dot(own_rest, back_in, NT)
    n_first, n_rows, _ = out_ref.shape
    cols = total_ref.shape[0] // n_first
    total = total_ref[...].astype(BF16).reshape(n_first, cols * part, LANES)
    out_ref[:, : cols * part] = total
    sent = halves(weight_part)
    spot = cols * part
    for value in sent:
        for j in range(value.shape[1] // LANES):
            piece = value[:, j * LANES : (j + 1) * LANES]
            for n in range(n_first):
                out_ref[n, spot : spot + part] = piece
            spot += part


def relay_kernel(got_ref, out_ref, *, own):
    n_peer = out_ref.shape[0]
    total = got_ref[0].astype(F32)
    for n in range(1, got_ref.shape[0]):
        total = total + got_ref[n].astype(F32)
    out_ref[:, :own] = total[: n_peer * own].astype(BF16).reshape(n_peer, own, LANES)
    value = total[n_peer * own :]
    half = value.shape[0] // 2
    head, rest = halves(value[:half] + value[half:])
    for n in range(n_peer):
        out_ref[n, own : own + half] = head
        out_ref[n, own + half :] = rest


def end_kernel(got_ref, norm_ref, grad_ref, weight_ref):
    total = got_ref[0].astype(F32)
    for n in range(1, got_ref.shape[0]):
        total = total + got_ref[n].astype(F32)
    part = grad_ref.shape[0]
    spot = 0
    for i in range(grad_ref.shape[1] // LANES):
        cut = slice(i * LANES, (i + 1) * LANES)
        grad_ref[:, cut] = (total[spot : spot + part] * norm_ref[:, cut]).astype(BF16)
        spot += part
    half = (total.shape[0] - spot) // 2
    for j in range(weight_ref.shape[1] // LANES):
        weight_ref[:, j * LANES : (j + 1) * LANES] = (
            total[spot : spot + part] + total[spot + half : spot + half + part]
        )
        spot += part


SMEM = pl.BlockSpec(memory_space=pltpu.SMEM)
VMEM = pl.BlockSpec(memory_space=pltpu.VMEM)
SCOPED = pltpu.CompilerParams(vmem_limit_bytes=24 * 2**20)


def call(kernel, outs, in_specs, *args, scratch=()):
    return pl.pallas_call(
        kernel,
        out_shape=outs,
        in_specs=in_specs,
        out_specs=jax.tree.map(lambda _: VMEM, outs),
        scratch_shapes=list(scratch),
        compiler_params=SCOPED,
    )(*args)


def per_device(features, weight, norm_scale, tile_rows, tile_cols, tile_vals, cotangent):
    rows_dev, part = features.shape
    tile_len = tile_vals.shape[1]
    row_tiles = rows_dev // tile_len
    hid_part = cotangent.shape[1]
    hidden = weight.shape[1]
    n_first = lax.axis_size(FIRST)
    n_second = lax.axis_size(SECOND)
    n_feat = lax.axis_size(FEAT)
    col_tiles = n_first * n_second * row_tiles
    norm = norm_scale.reshape(1, rows_dev)
    shape = jax.ShapeDtypeStruct

    block = call(
        start_kernel,
        shape((n_second, row_tiles, part, tile_len), BF16),
        [VMEM, VMEM],
        features.T,
        norm,
    )
    block = lax.all_to_all(block, SECOND, 0, 0)
    block = lax.all_to_all(
        jnp.broadcast_to(block[None], (n_first,) + block.shape), FIRST, 0, 0
    )
    group = call(
        forward_kernel,
        shape((n_feat, 3 * part + hid_part, rows_dev), BF16),
        [SMEM, SMEM, VMEM, VMEM, VMEM, VMEM],
        tile_rows,
        tile_cols,
        tile_vals,
        block.reshape(col_tiles, part, tile_len),
        weight,
        cotangent.T,
    )
    group = lax.all_to_all(group, FEAT, 0, 0)
    own = row_tiles * part
    weight_rows = 2 * part * hidden // tile_len
    activated, sent = call(
        middle_kernel,
        (
            shape((hid_part, rows_dev), BF16),
            shape((n_first, n_second * own + weight_rows, tile_len), BF16),
        ),
        [SMEM, SMEM, VMEM, VMEM, VMEM, VMEM],
        tile_rows,
        tile_cols,
        tile_vals,
        group,
        weight,
        norm,
        scratch=(
            pltpu.VMEM((hidden, rows_dev), F32),
            pltpu.VMEM((col_tiles, part, tile_len), F32),
        ),
    )
    got = lax.all_to_all(sent, FIRST, 0, 0)
    sent = call(
        functools.partial(relay_kernel, own=own),
        shape((n_second, own + weight_rows, tile_len), BF16),
        [VMEM],
        got,
    )
    got = lax.all_to_all(sent, SECOND, 0, 0)
    feature_grad, weight_grad = call(
        end_kernel,
        (shape((part, rows_dev), BF16), shape((part, hidden), F32)),
        [VMEM, VMEM],
        got,
        norm,
    )
    return (activated.T, weight_grad, feature_grad.T)


FIRST, SECOND, FEAT = ("x", "z"), "y", "feat"


def axes_of(rows):
    return (4, 8, 3) if rows == 96 else (2, rows // 4, 2)


def solution(mesh):
    fine = Mesh(
        mesh.devices.reshape(axes_of(mesh.shape["row"]) + (mesh.shape["feat"],)), ("x", "y", "z", "feat")
    )
    row = ("x", "y", "z")
    placed = (
        P(row, "feat"),
        P("feat", None),
        P(row),
        P(row),
        P(row),
        P(row, None, None),
        P(row, "feat"),
    )
    return jax.shard_map(
        per_device,
        mesh=fine,
        in_specs=placed,
        out_specs=(P(row, "feat"), P("feat", None), P(row, "feat")),
        check_vma=False,
    )
```

```python
import functools

import jax
import jax.numpy as jnp
from jax import lax
from jax.experimental import pallas as pl
from jax.experimental.pallas import tpu as pltpu
from jax.sharding import Mesh, PartitionSpec as P

F32 = jnp.float32
BF16 = jnp.bfloat16
NT = (((1,), (1,)), ((), ()))
NN = (((1,), (0,)), ((), ()))
TN = (((0,), (0,)), ((), ()))
LANES = 128


def halves(value):
    head = value.astype(BF16)
    return head, (value - head.astype(F32)).astype(BF16)


def dot(left, right, dims):
    return lax.dot_general(left, right, dims, preferred_element_type=F32)


def spot_of(tile, row_tiles):
    n_z, n_y = lax.axis_size("z"), lax.axis_size("y")
    within, owner = lax.rem(tile, row_tiles), lax.div(tile, row_tiles)
    z, owner = lax.rem(owner, n_z), lax.div(owner, n_z)
    y, x = lax.rem(owner, n_y), lax.div(owner, n_y)
    return (x * n_z + z) * n_y + y, within


def forward_kernel(rows_ref, cols_ref, tiles_ref, nodes_ref, weight_ref, cot_ref, out_ref):
    part = weight_ref.shape[0]
    row_tiles = cot_ref.shape[1] // LANES
    totals = [jnp.zeros((part, LANES), F32) for _ in range(row_tiles)]
    for t in range(tiles_ref.shape[0]):
        owner, within = spot_of(cols_ref[t], row_tiles)
        nodes = nodes_ref[owner, :, pl.ds(pl.multiple_of(within * LANES, LANES), LANES)]
        term = dot(nodes, tiles_ref[t], NT)
        for i in range(row_tiles):
            totals[i] = totals[i] + jnp.where(rows_ref[t] == i, term, 0.0)
    for i in range(row_tiles):
        head, rest = halves(totals[i])
        cut = slice(i * LANES, (i + 1) * LANES)
        for n in range(out_ref.shape[0]):
            out_ref[n, 0:part, cut] = head
            out_ref[n, part : 2 * part, cut] = rest
    for n in range(out_ref.shape[0]):
        out_ref[n, 2 * part : 3 * part] = weight_ref[...]
        out_ref[n, 3 * part :] = cot_ref[...]


def middle_kernel(
    rows_ref, cols_ref, tiles_ref, group_ref, weight_ref, norm_ref, act_ref, out_ref, pre_ref, total_ref
):
    my_zh, my_core = lax.axis_index("zh"), lax.axis_index("core")
    n_zh, n_core = lax.axis_size("zh"), lax.axis_size("core")
    me, my_place = my_zh * n_core + my_core, my_core * n_zh + my_zh
    part = weight_ref.shape[0]
    hid_part = act_ref.shape[0]
    n_feat = group_ref.shape[0]
    group = group_ref[...]
    head = group[:, 0:part].reshape(n_feat * part, -1)
    rest = group[:, part : 2 * part].reshape(n_feat * part, -1)
    weight_all = group[:, 2 * part : 3 * part].reshape(n_feat * part, -1)
    cot = jnp.concatenate(
        [group[core * n_zh + zh, 3 * part :] for zh in range(n_zh) for core in range(n_core)], axis=0
    )
    norm = norm_ref[...]
    pre = (dot(weight_all, head, TN) + dot(weight_all, rest, TN)) * norm
    pre_ref[...] = pre
    sigma = 1.0 / (1.0 + jnp.exp(-pre))
    slope = sigma * (1.0 + pre * (1.0 - sigma))
    back_in = (cot.astype(F32) * slope * norm).astype(BF16)
    own = pre_ref[pl.ds(pl.multiple_of(me * hid_part, hid_part), hid_part)]
    act_ref[...] = (own / (1.0 + jnp.exp(-own))).astype(BF16)

    back = dot(weight_ref[...], back_in, NN)
    row_tiles = back.shape[1] // LANES
    back_head, back_rest = halves(back)
    back_tiles = [
        jnp.concatenate([h[:, i * LANES : (i + 1) * LANES] for h in (back_head, back_rest)], axis=0)
        for i in range(row_tiles)
    ]
    total_ref[...] = jnp.zeros_like(total_ref)
    for t in range(tiles_ref.shape[0]):
        left = back_tiles[0]
        for i in range(1, row_tiles):
            left = jnp.where(rows_ref[t] == i, back_tiles[i], left)
        both = dot(left, tiles_ref[t], NN)
        owner, within = spot_of(cols_ref[t], row_tiles)
        total_ref[owner * row_tiles + within] += both[:part] + both[part:]

    own_head = group_ref[pl.ds(my_place, 1), 0:part][0]
    own_rest = group_ref[pl.ds(my_place, 1), part : 2 * part][0]
    weight_part = dot(own_head, back_in, NT) + dot(own_rest, back_in, NT)
    n_first, n_rows, _ = out_ref.shape
    cols = total_ref.shape[0] // n_first
    total = total_ref[...].astype(BF16).reshape(n_first, cols * part, LANES)
    out_ref[:, : cols * part] = total
    weight_part = weight_part.astype(BF16)
    spot = cols * part
    for j in range(weight_part.shape[1] // LANES):
        for n in range(n_first):
            out_ref[n, spot : spot + part] = weight_part[:, j * LANES : (j + 1) * LANES]
        spot += part


def relay_kernel(got_ref, out_ref, *, own):
    n_peer = out_ref.shape[0]
    total = got_ref[0].astype(F32)
    for n in range(1, got_ref.shape[0]):
        total = total + got_ref[n].astype(F32)
    out_ref[:, :own] = total[: n_peer * own].astype(BF16).reshape(n_peer, own, LANES)
    for n in range(n_peer):
        out_ref[n, own:] = total[n_peer * own :].astype(BF16)


def end_kernel(got_ref, norm_ref, grad_ref, weight_ref):
    total = got_ref[0].astype(F32)
    for n in range(1, got_ref.shape[0]):
        total = total + got_ref[n].astype(F32)
    part = grad_ref.shape[0]
    spot = 0
    for i in range(grad_ref.shape[1] // LANES):
        cut = slice(i * LANES, (i + 1) * LANES)
        grad_ref[:, cut] = (total[spot : spot + part] * norm_ref[:, cut]).astype(BF16)
        spot += part
    for j in range(weight_ref.shape[1] // LANES):
        weight_ref[:, j * LANES : (j + 1) * LANES] = total[spot : spot + part]
        spot += part


SMEM = pl.BlockSpec(memory_space=pltpu.SMEM)
VMEM = pl.BlockSpec(memory_space=pltpu.VMEM)
SCOPED = pltpu.CompilerParams(vmem_limit_bytes=24 * 2**20)


def call(kernel, outs, in_specs, *args, scratch=()):
    return pl.pallas_call(
        kernel,
        out_shape=outs,
        in_specs=in_specs,
        out_specs=jax.tree.map(lambda _: VMEM, outs),
        scratch_shapes=list(scratch),
        compiler_params=SCOPED,
    )(*args)


def per_device(features, weight, norm_scale, tile_rows, tile_cols, tile_vals, cotangent):
    rows_dev, part = features.shape
    tile_len = tile_vals.shape[1]
    row_tiles = rows_dev // tile_len
    hid_part = cotangent.shape[1]
    hidden = weight.shape[1]
    n_first = lax.axis_size(FIRST)
    n_second = lax.axis_size(SECOND)
    col_tiles = n_first * n_second * row_tiles
    norm = norm_scale.reshape(1, rows_dev)
    shape = jax.ShapeDtypeStruct

    block = (features.T.astype(F32) * norm_scale[None, :]).astype(BF16)
    block = jnp.broadcast_to(block[None], (n_second,) + block.shape)
    block = lax.all_to_all(block, SECOND, 0, 0)
    block = lax.all_to_all(
        jnp.broadcast_to(block[None], (n_first,) + block.shape), FIRST, 0, 0
    )
    group = call(
        forward_kernel,
        shape((lax.axis_size("zh"), 3 * part + hid_part, rows_dev), BF16),
        [SMEM, SMEM, VMEM, VMEM, VMEM, VMEM],
        tile_rows,
        tile_cols,
        tile_vals,
        block.reshape(n_first * n_second, part, rows_dev),
        weight,
        cotangent.T,
    )
    group = lax.all_gather(lax.all_to_all(group, "zh", 0, 0), "core", axis=0, tiled=True)
    own = row_tiles * part
    weight_rows = part * hidden // tile_len
    activated, sent = call(
        middle_kernel,
        (
            shape((hid_part, rows_dev), BF16),
            shape((n_first, n_second * own + weight_rows, tile_len), BF16),
        ),
        [SMEM, SMEM, VMEM, VMEM, VMEM, VMEM],
        tile_rows,
        tile_cols,
        tile_vals,
        group,
        weight,
        norm,
        scratch=(
            pltpu.VMEM((hidden, rows_dev), F32),
            pltpu.VMEM((col_tiles, part, tile_len), F32),
        ),
    )
    got = lax.all_to_all(sent, FIRST, 0, 0)
    sent = call(
        functools.partial(relay_kernel, own=own),
        shape((n_second, own + weight_rows, tile_len), BF16),
        [VMEM],
        got,
    )
    got = lax.all_to_all(sent, SECOND, 0, 0)
    feature_grad, weight_grad = call(
        end_kernel,
        (shape((part, rows_dev), BF16), shape((part, hidden), F32)),
        [VMEM, VMEM],
        got,
        norm,
    )
    return (activated.T, weight_grad, feature_grad.T)


FIRST, SECOND = ("x", "z"), "y"


def axes_of(rows, feats):
    return ((4, 8, 3) if rows == 96 else (2, rows // 4, 2)) + (feats // 2, 2)


def solution(mesh):
    sizes = axes_of(mesh.shape["row"], mesh.shape["feat"])
    fine = Mesh(mesh.devices.reshape(sizes), ("x", "y", "z", "zh", "core"))
    row, feat = ("x", "y", "z"), ("zh", "core")
    placed = (
        P(row, feat),
        P(feat, None),
        P(row),
        P(row),
        P(row),
        P(row, None, None),
        P(row, feat),
    )
    return jax.shard_map(
        per_device,
        mesh=fine,
        in_specs=placed,
        out_specs=(P(row, feat), P(feat, None), P(row, feat)),
        check_vma=False,
    )
```

```python
import functools

import jax
import jax.numpy as jnp
from jax import lax
from jax.experimental import pallas as pl
from jax.experimental.pallas import tpu as pltpu
from jax.sharding import Mesh, PartitionSpec as P

F32 = jnp.float32
BF16 = jnp.bfloat16
NT = (((1,), (1,)), ((), ()))
NN = (((1,), (0,)), ((), ()))
TN = (((0,), (0,)), ((), ()))
LANES = 128


def halves(value):
    head = value.astype(BF16)
    return head, (value - head.astype(F32)).astype(BF16)


def dot(left, right, dims):
    return lax.dot_general(left, right, dims, preferred_element_type=F32)


def spot_of(tile, row_tiles):
    n_z, n_y = lax.axis_size("z"), lax.axis_size("y")
    within, owner = lax.rem(tile, row_tiles), lax.div(tile, row_tiles)
    z, owner = lax.rem(owner, n_z), lax.div(owner, n_z)
    y, x = lax.rem(owner, n_y), lax.div(owner, n_y)
    return (x * n_z + z) * n_y + y, within


def forward_kernel(rows_ref, cols_ref, tiles_ref, nodes_ref, weight_ref, cot_ref, out_ref):
    part = weight_ref.shape[0]
    row_tiles = cot_ref.shape[1] // LANES
    totals = [jnp.zeros((part, LANES), F32) for _ in range(row_tiles)]
    for t in range(tiles_ref.shape[0]):
        owner, within = spot_of(cols_ref[t], row_tiles)
        nodes = nodes_ref[owner, :, pl.ds(pl.multiple_of(within * LANES, LANES), LANES)]
        term = dot(nodes, tiles_ref[t], NT)
        for i in range(row_tiles):
            totals[i] = totals[i] + jnp.where(rows_ref[t] == i, term, 0.0)
    for i in range(row_tiles):
        value = totals[i].astype(BF16)
        for n in range(out_ref.shape[0]):
            out_ref[n, 0:part, i * LANES : (i + 1) * LANES] = value
    for n in range(out_ref.shape[0]):
        out_ref[n, part : 2 * part] = weight_ref[...]
        out_ref[n, 2 * part :] = cot_ref[...]


def middle_kernel(
    rows_ref, cols_ref, tiles_ref, held_ref, came_ref, weight_ref, norm_ref, act_ref, out_ref, pre_ref, total_ref
):
    my_zh, my_core = lax.axis_index("zh"), lax.axis_index("core")
    n_zh, n_core = lax.axis_size("zh"), lax.axis_size("core")
    me = my_zh * n_core + my_core
    part = weight_ref.shape[0]
    hid_part = act_ref.shape[0]
    held, came = held_ref[...], came_ref[...]

    def both(cut):
        return jnp.concatenate([g[zh, cut] for g in (held, came) for zh in range(n_zh)], axis=0)

    mixed = both(slice(0, part))
    weight_all = both(slice(part, 2 * part))
    low = my_core == 0
    cot = jnp.concatenate(
        [
            value
            for zh in range(n_zh)
            for h, c in [(held[zh, 2 * part :], came[zh, 2 * part :])]
            for value in (jnp.where(low, h, c), jnp.where(low, c, h))
        ],
        axis=0,
    )
    norm = norm_ref[...]
    pre = dot(weight_all, mixed, TN) * norm
    pre_ref[...] = pre
    sigma = 1.0 / (1.0 + jnp.exp(-pre))
    slope = sigma * (1.0 + pre * (1.0 - sigma))
    back_in = (cot.astype(F32) * slope * norm).astype(BF16)
    own = pre_ref[pl.ds(pl.multiple_of(me * hid_part, hid_part), hid_part)]
    act_ref[...] = (own / (1.0 + jnp.exp(-own))).astype(BF16)

    back = dot(weight_ref[...], back_in, NN)
    row_tiles = back.shape[1] // LANES
    back_head, back_rest = halves(back)
    back_tiles = [
        jnp.concatenate([h[:, i * LANES : (i + 1) * LANES] for h in (back_head, back_rest)], axis=0)
        for i in range(row_tiles)
    ]
    total_ref[...] = jnp.zeros_like(total_ref)
    for t in range(tiles_ref.shape[0]):
        left = back_tiles[0]
        for i in range(1, row_tiles):
            left = jnp.where(rows_ref[t] == i, back_tiles[i], left)
        both = dot(left, tiles_ref[t], NN)
        owner, within = spot_of(cols_ref[t], row_tiles)
        total_ref[owner * row_tiles + within] += both[:part] + both[part:]

    weight_part = dot(held_ref[pl.ds(my_zh, 1), 0:part][0], back_in, NT)
    n_first, n_rows, _ = out_ref.shape
    cols = total_ref.shape[0] // n_first
    total = total_ref[...].astype(BF16).reshape(n_first, cols * part, LANES)
    out_ref[:, : cols * part] = total
    weight_part = weight_part.astype(BF16)
    spot = cols * part
    for j in range(weight_part.shape[1] // LANES):
        for n in range(n_first):
            out_ref[n, spot : spot + part] = weight_part[:, j * LANES : (j + 1) * LANES]
        spot += part


def relay_kernel(got_ref, out_ref, *, own):
    n_peer = out_ref.shape[0]
    total = got_ref[0].astype(F32)
    for n in range(1, got_ref.shape[0]):
        total = total + got_ref[n].astype(F32)
    out_ref[:, :own] = total[: n_peer * own].astype(BF16).reshape(n_peer, own, LANES)
    for n in range(n_peer):
        out_ref[n, own:] = total[n_peer * own :].astype(BF16)


def end_kernel(got_ref, norm_ref, grad_ref, weight_ref):
    total = got_ref[0].astype(F32)
    for n in range(1, got_ref.shape[0]):
        total = total + got_ref[n].astype(F32)
    part = grad_ref.shape[0]
    spot = 0
    for i in range(grad_ref.shape[1] // LANES):
        cut = slice(i * LANES, (i + 1) * LANES)
        grad_ref[:, cut] = (total[spot : spot + part] * norm_ref[:, cut]).astype(BF16)
        spot += part
    for j in range(weight_ref.shape[1] // LANES):
        weight_ref[:, j * LANES : (j + 1) * LANES] = total[spot : spot + part]
        spot += part


SMEM = pl.BlockSpec(memory_space=pltpu.SMEM)
VMEM = pl.BlockSpec(memory_space=pltpu.VMEM)
SCOPED = pltpu.CompilerParams(vmem_limit_bytes=24 * 2**20)


def call(kernel, outs, in_specs, *args, scratch=()):
    return pl.pallas_call(
        kernel,
        out_shape=outs,
        in_specs=in_specs,
        out_specs=jax.tree.map(lambda _: VMEM, outs),
        scratch_shapes=list(scratch),
        compiler_params=SCOPED,
    )(*args)


def per_device(features, weight, norm_scale, tile_rows, tile_cols, tile_vals, cotangent):
    rows_dev, part = features.shape
    tile_len = tile_vals.shape[1]
    row_tiles = rows_dev // tile_len
    hid_part = cotangent.shape[1]
    hidden = weight.shape[1]
    n_first = lax.axis_size(FIRST)
    n_second = lax.axis_size(SECOND)
    col_tiles = n_first * n_second * row_tiles
    norm = norm_scale.reshape(1, rows_dev)
    shape = jax.ShapeDtypeStruct

    block = (features.T.astype(F32) * norm_scale[None, :]).astype(BF16)
    block = jnp.broadcast_to(block[None], (n_second,) + block.shape)
    block = lax.all_to_all(block, SECOND, 0, 0)
    block = lax.all_to_all(
        jnp.broadcast_to(block[None], (n_first,) + block.shape), FIRST, 0, 0
    )
    group = call(
        forward_kernel,
        shape((lax.axis_size("zh"), 2 * part + hid_part, rows_dev), BF16),
        [SMEM, SMEM, VMEM, VMEM, VMEM, VMEM],
        tile_rows,
        tile_cols,
        tile_vals,
        block.reshape(n_first * n_second, part, rows_dev),
        weight,
        cotangent.T,
    )
    held = lax.all_to_all(group, "zh", 0, 0)
    came = lax.ppermute(held, "core", [(0, 1), (1, 0)])
    own = row_tiles * part
    weight_rows = part * hidden // tile_len
    activated, sent = call(
        middle_kernel,
        (
            shape((hid_part, rows_dev), BF16),
            shape((n_first, n_second * own + weight_rows, tile_len), BF16),
        ),
        [SMEM, SMEM, VMEM, VMEM, VMEM, VMEM, VMEM],
        tile_rows,
        tile_cols,
        tile_vals,
        held,
        came,
        weight,
        norm,
        scratch=(
            pltpu.VMEM((hidden, rows_dev), F32),
            pltpu.VMEM((col_tiles, part, tile_len), F32),
        ),
    )
    got = lax.all_to_all(sent, FIRST, 0, 0)
    sent = call(
        functools.partial(relay_kernel, own=own),
        shape((n_second, own + weight_rows, tile_len), BF16),
        [VMEM],
        got,
    )
    got = lax.all_to_all(sent, SECOND, 0, 0)
    feature_grad, weight_grad = call(
        end_kernel,
        (shape((part, rows_dev), BF16), shape((part, hidden), F32)),
        [VMEM, VMEM],
        got,
        norm,
    )
    return (activated.T, weight_grad, feature_grad.T)


FIRST, SECOND = ("x", "z"), "y"


def axes_of(rows, feats):
    return ((4, 8, 3) if rows == 96 else (2, rows // 4, 2)) + (feats // 2, 2)


def solution(mesh):
    sizes = axes_of(mesh.shape["row"], mesh.shape["feat"])
    fine = Mesh(mesh.devices.reshape(sizes), ("x", "y", "z", "zh", "core"))
    row, feat = ("x", "y", "z"), ("zh", "core")
    placed = (
        P(row, feat),
        P(feat, None),
        P(row),
        P(row),
        P(row),
        P(row, None, None),
        P(row, feat),
    )
    return jax.shard_map(
        per_device,
        mesh=fine,
        in_specs=placed,
        out_specs=(P(row, feat), P(feat, None), P(row, feat)),
        check_vma=False,
    )
```

```python
import functools

import jax
import jax.numpy as jnp
from jax import lax
from jax.experimental import pallas as pl
from jax.experimental.pallas import tpu as pltpu
from jax.sharding import Mesh, PartitionSpec as P

F32 = jnp.float32
BF16 = jnp.bfloat16
NT = (((1,), (1,)), ((), ()))
NN = (((1,), (0,)), ((), ()))
TN = (((0,), (0,)), ((), ()))
LANES = 128


def halves(value):
    head = value.astype(BF16)
    return head, (value - head.astype(F32)).astype(BF16)


def dot(left, right, dims):
    return lax.dot_general(left, right, dims, preferred_element_type=F32)


def spot_of(tile, row_tiles):
    n_z, n_y = lax.axis_size("z"), lax.axis_size("y")
    within, owner = lax.rem(tile, row_tiles), lax.div(tile, row_tiles)
    z, owner = lax.rem(owner, n_z), lax.div(owner, n_z)
    y, x = lax.rem(owner, n_y), lax.div(owner, n_y)
    return (x * n_z + z) * n_y + y, within


def forward_kernel(rows_ref, cols_ref, tiles_ref, nodes_ref, weight_ref, cot_ref, out_ref):
    part = weight_ref.shape[0]
    row_tiles = cot_ref.shape[1] // LANES
    totals = [jnp.zeros((part, LANES), F32) for _ in range(row_tiles)]
    for t in range(tiles_ref.shape[0]):
        owner, within = lax.div(cols_ref[t], row_tiles), lax.rem(cols_ref[t], row_tiles)
        nodes = nodes_ref[owner, :, pl.ds(pl.multiple_of(within * LANES, LANES), LANES)]
        term = dot(nodes, tiles_ref[t], NT)
        for i in range(row_tiles):
            totals[i] = totals[i] + jnp.where(rows_ref[t] == i, term, 0.0)
    for i in range(row_tiles):
        head, rest = halves(totals[i])
        cut = slice(i * LANES, (i + 1) * LANES)
        for n in range(out_ref.shape[0]):
            out_ref[n, 0:part, cut] = head
            out_ref[n, part : 2 * part, cut] = rest
    for n in range(out_ref.shape[0]):
        out_ref[n, 2 * part : 3 * part] = weight_ref[...]
        out_ref[n, 3 * part :] = cot_ref[...]


def middle_kernel(
    rows_ref, cols_ref, tiles_ref, group_ref, weight_ref, norm_ref, act_ref, out_ref, pre_ref, total_ref
):
    my_zh, my_core = lax.axis_index("zh"), lax.axis_index("core")
    n_zh, n_core = lax.axis_size("zh"), lax.axis_size("core")
    me, my_place = my_zh * n_core + my_core, my_core * n_zh + my_zh
    part = weight_ref.shape[0]
    hid_part = act_ref.shape[0]
    n_feat = group_ref.shape[0]
    group = group_ref[...]
    head = group[:, 0:part].reshape(n_feat * part, -1)
    rest = group[:, part : 2 * part].reshape(n_feat * part, -1)
    weight_all = group[:, 2 * part : 3 * part].reshape(n_feat * part, -1)
    cot = jnp.concatenate(
        [group[core * n_zh + zh, 3 * part :] for zh in range(n_zh) for core in range(n_core)], axis=0
    )
    norm = norm_ref[...]
    pre = (dot(weight_all, head, TN) + dot(weight_all, rest, TN)) * norm
    pre_ref[...] = pre
    sigma = 1.0 / (1.0 + jnp.exp(-pre))
    slope = sigma * (1.0 + pre * (1.0 - sigma))
    back_in = (cot.astype(F32) * slope * norm).astype(BF16)
    own = pre_ref[pl.ds(pl.multiple_of(me * hid_part, hid_part), hid_part)]
    act_ref[...] = (own / (1.0 + jnp.exp(-own))).astype(BF16)

    back = dot(weight_ref[...], back_in, NN)
    row_tiles = back.shape[1] // LANES
    back_head, back_rest = halves(back)
    back_tiles = [
        jnp.concatenate([h[:, i * LANES : (i + 1) * LANES] for h in (back_head, back_rest)], axis=0)
        for i in range(row_tiles)
    ]
    total_ref[...] = jnp.zeros_like(total_ref)
    for t in range(tiles_ref.shape[0]):
        left = back_tiles[0]
        for i in range(1, row_tiles):
            left = jnp.where(rows_ref[t] == i, back_tiles[i], left)
        both = dot(left, tiles_ref[t], NN)
        owner, within = spot_of(cols_ref[t], row_tiles)
        total_ref[owner * row_tiles + within] += both[:part] + both[part:]

    own_head = group_ref[pl.ds(my_place, 1), 0:part][0]
    own_rest = group_ref[pl.ds(my_place, 1), part : 2 * part][0]
    weight_part = dot(own_head, back_in, NT) + dot(own_rest, back_in, NT)
    n_first, n_rows, _ = out_ref.shape
    cols = total_ref.shape[0] // n_first
    total = total_ref[...].astype(BF16).reshape(n_first, cols * part, LANES)
    out_ref[:, : cols * part] = total
    weight_part = weight_part.astype(BF16)
    spot = cols * part
    for j in range(weight_part.shape[1] // LANES):
        for n in range(n_first):
            out_ref[n, spot : spot + part] = weight_part[:, j * LANES : (j + 1) * LANES]
        spot += part


def relay_kernel(got_ref, out_ref, *, own):
    n_peer = out_ref.shape[0]
    total = got_ref[0].astype(F32)
    for n in range(1, got_ref.shape[0]):
        total = total + got_ref[n].astype(F32)
    out_ref[:, :own] = total[: n_peer * own].astype(BF16).reshape(n_peer, own, LANES)
    for n in range(n_peer):
        out_ref[n, own:] = total[n_peer * own :].astype(BF16)


def end_kernel(got_ref, norm_ref, grad_ref, weight_ref):
    total = got_ref[0].astype(F32)
    for n in range(1, got_ref.shape[0]):
        total = total + got_ref[n].astype(F32)
    part = grad_ref.shape[0]
    spot = 0
    for i in range(grad_ref.shape[1] // LANES):
        cut = slice(i * LANES, (i + 1) * LANES)
        grad_ref[:, cut] = (total[spot : spot + part] * norm_ref[:, cut]).astype(BF16)
        spot += part
    for j in range(weight_ref.shape[1] // LANES):
        weight_ref[:, j * LANES : (j + 1) * LANES] = total[spot : spot + part]
        spot += part


SMEM = pl.BlockSpec(memory_space=pltpu.SMEM)
VMEM = pl.BlockSpec(memory_space=pltpu.VMEM)
SCOPED = pltpu.CompilerParams(vmem_limit_bytes=24 * 2**20)


def call(kernel, outs, in_specs, *args, scratch=()):
    return pl.pallas_call(
        kernel,
        out_shape=outs,
        in_specs=in_specs,
        out_specs=jax.tree.map(lambda _: VMEM, outs),
        scratch_shapes=list(scratch),
        compiler_params=SCOPED,
    )(*args)


def per_device(features, weight, norm_scale, tile_rows, tile_cols, tile_vals, cotangent):
    rows_dev, part = features.shape
    tile_len = tile_vals.shape[1]
    row_tiles = rows_dev // tile_len
    hid_part = cotangent.shape[1]
    hidden = weight.shape[1]
    n_first = lax.axis_size(FIRST)
    n_second = lax.axis_size(SECOND)
    col_tiles = n_first * n_second * row_tiles
    norm = norm_scale.reshape(1, rows_dev)
    shape = jax.ShapeDtypeStruct

    block = (features.T.astype(F32) * norm_scale[None, :]).astype(BF16)
    for axes in OUT:
        block = jnp.broadcast_to(block[None], (lax.axis_size(axes),) + block.shape)
        block = lax.all_to_all(block, axes, 0, 0)
    group = call(
        forward_kernel,
        shape((lax.axis_size("zh"), 3 * part + hid_part, rows_dev), BF16),
        [SMEM, SMEM, VMEM, VMEM, VMEM, VMEM],
        tile_rows,
        tile_cols,
        tile_vals,
        block.reshape(n_first * n_second, part, rows_dev),
        weight,
        cotangent.T,
    )
    group = lax.all_gather(lax.all_to_all(group, "zh", 0, 0), "core", axis=0, tiled=True)
    own = row_tiles * part
    weight_rows = part * hidden // tile_len
    activated, sent = call(
        middle_kernel,
        (
            shape((hid_part, rows_dev), BF16),
            shape((n_first, n_second * own + weight_rows, tile_len), BF16),
        ),
        [SMEM, SMEM, VMEM, VMEM, VMEM, VMEM],
        tile_rows,
        tile_cols,
        tile_vals,
        group,
        weight,
        norm,
        scratch=(
            pltpu.VMEM((hidden, rows_dev), F32),
            pltpu.VMEM((col_tiles, part, tile_len), F32),
        ),
    )
    got = lax.all_to_all(sent, FIRST, 0, 0)
    sent = call(
        functools.partial(relay_kernel, own=own),
        shape((n_second, own + weight_rows, tile_len), BF16),
        [VMEM],
        got,
    )
    got = lax.all_to_all(sent, SECOND, 0, 0)
    feature_grad, weight_grad = call(
        end_kernel,
        (shape((part, rows_dev), BF16), shape((part, hidden), F32)),
        [VMEM, VMEM],
        got,
        norm,
    )
    return (activated.T, weight_grad, feature_grad.T)


OUT = (("y", "z"), "x")
FIRST, SECOND = ("x", "z"), "y"


def axes_of(rows, feats):
    return ((4, 8, 3) if rows == 96 else (2, rows // 4, 2)) + (feats // 2, 2)


def solution(mesh):
    sizes = axes_of(mesh.shape["row"], mesh.shape["feat"])
    fine = Mesh(mesh.devices.reshape(sizes), ("x", "y", "z", "zh", "core"))
    row, feat = ("x", "y", "z"), ("zh", "core")
    placed = (
        P(row, feat),
        P(feat, None),
        P(row),
        P(row),
        P(row),
        P(row, None, None),
        P(row, feat),
    )
    return jax.shard_map(
        per_device,
        mesh=fine,
        in_specs=placed,
        out_specs=(P(row, feat), P(feat, None), P(row, feat)),
        check_vma=False,
    )
```

```python
import functools

import jax
import jax.numpy as jnp
from jax import lax
from jax.experimental import pallas as pl
from jax.experimental.pallas import tpu as pltpu
from jax.sharding import Mesh, PartitionSpec as P

F32 = jnp.float32
BF16 = jnp.bfloat16
NT = (((1,), (1,)), ((), ()))
NN = (((1,), (0,)), ((), ()))
TN = (((0,), (0,)), ((), ()))
LANES = 128


def halves(value):
    head = value.astype(BF16)
    return head, (value - head.astype(F32)).astype(BF16)


def dot(left, right, dims):
    return lax.dot_general(left, right, dims, preferred_element_type=F32)


def spot_of(tile, row_tiles):
    n_z, n_y = lax.axis_size("z"), lax.axis_size("y")
    within, owner = lax.rem(tile, row_tiles), lax.div(tile, row_tiles)
    z, owner = lax.rem(owner, n_z), lax.div(owner, n_z)
    y, x = lax.rem(owner, n_y), lax.div(owner, n_y)
    return (x * n_z + z) * n_y + y, within


def forward_kernel(rows_ref, cols_ref, tiles_ref, nodes_ref, weight_ref, cot_ref, out_ref):
    part = weight_ref.shape[0]
    row_tiles = cot_ref.shape[1] // LANES
    sums = jnp.zeros((row_tiles * part, LANES), F32)
    for t in range(0, tiles_ref.shape[0], 2):
        lefts = []
        for u in (t, t + 1):
            owner, within = lax.div(cols_ref[u], row_tiles), lax.rem(cols_ref[u], row_tiles)
            nodes = nodes_ref[owner, :, pl.ds(pl.multiple_of(within * LANES, LANES), LANES)]
            none = jnp.zeros_like(nodes)
            lefts.append(
                jnp.concatenate([jnp.where(rows_ref[u] == i, nodes, none) for i in range(row_tiles)], axis=0)
            )
        right = jnp.concatenate([tiles_ref[t], tiles_ref[t + 1]], axis=1)
        sums = sums + dot(jnp.concatenate(lefts, axis=1), right, NT)
    totals = [sums[i * part : (i + 1) * part] for i in range(row_tiles)]
    for i in range(row_tiles):
        head, rest = halves(totals[i])
        cut = slice(i * LANES, (i + 1) * LANES)
        for n in range(out_ref.shape[0]):
            out_ref[n, 0:part, cut] = head
            out_ref[n, part : 2 * part, cut] = rest
    for n in range(out_ref.shape[0]):
        out_ref[n, 2 * part : 3 * part] = weight_ref[...]
        out_ref[n, 3 * part :] = cot_ref[...]


def middle_kernel(
    rows_ref, cols_ref, tiles_ref, group_ref, weight_ref, norm_ref, act_ref, out_ref, pre_ref, total_ref
):
    my_zh, my_core = lax.axis_index("zh"), lax.axis_index("core")
    n_zh, n_core = lax.axis_size("zh"), lax.axis_size("core")
    me, my_place = my_zh * n_core + my_core, my_core * n_zh + my_zh
    part = weight_ref.shape[0]
    hid_part = act_ref.shape[0]
    n_feat = group_ref.shape[0]
    group = group_ref[...]
    head = group[:, 0:part].reshape(n_feat * part, -1)
    rest = group[:, part : 2 * part].reshape(n_feat * part, -1)
    weight_all = group[:, 2 * part : 3 * part].reshape(n_feat * part, -1)
    cot = jnp.concatenate(
        [group[core * n_zh + zh, 3 * part :] for zh in range(n_zh) for core in range(n_core)], axis=0
    )
    norm = norm_ref[...]
    pre = (dot(weight_all, head, TN) + dot(weight_all, rest, TN)) * norm
    pre_ref[...] = pre
    sigma = 1.0 / (1.0 + jnp.exp(-pre))
    slope = sigma * (1.0 + pre * (1.0 - sigma))
    back_in = (cot.astype(F32) * slope * norm).astype(BF16)
    own = pre_ref[pl.ds(pl.multiple_of(me * hid_part, hid_part), hid_part)]
    act_ref[...] = (own / (1.0 + jnp.exp(-own))).astype(BF16)

    back = dot(weight_ref[...], back_in, NN)
    row_tiles = back.shape[1] // LANES
    back_head, back_rest = halves(back)
    back_tiles = [
        jnp.concatenate([h[:, i * LANES : (i + 1) * LANES] for h in (back_head, back_rest)], axis=0)
        for i in range(row_tiles)
    ]
    total_ref[...] = jnp.zeros_like(total_ref)
    for t in range(tiles_ref.shape[0]):
        left = back_tiles[0]
        for i in range(1, row_tiles):
            left = jnp.where(rows_ref[t] == i, back_tiles[i], left)
        both = dot(left, tiles_ref[t], NN)
        owner, within = spot_of(cols_ref[t], row_tiles)
        total_ref[owner * row_tiles + within] += both[:part] + both[part:]

    own_head = group_ref[pl.ds(my_place, 1), 0:part][0]
    own_rest = group_ref[pl.ds(my_place, 1), part : 2 * part][0]
    weight_part = dot(own_head, back_in, NT) + dot(own_rest, back_in, NT)
    n_first, n_rows, _ = out_ref.shape
    cols = total_ref.shape[0] // n_first
    total = total_ref[...].astype(BF16).reshape(n_first, cols * part, LANES)
    out_ref[:, : cols * part] = total
    weight_part = weight_part.astype(BF16)
    spot = cols * part
    for j in range(weight_part.shape[1] // LANES):
        for n in range(n_first):
            out_ref[n, spot : spot + part] = weight_part[:, j * LANES : (j + 1) * LANES]
        spot += part


def relay_kernel(got_ref, out_ref, *, own):
    n_peer = out_ref.shape[0]
    total = got_ref[0].astype(F32)
    for n in range(1, got_ref.shape[0]):
        total = total + got_ref[n].astype(F32)
    out_ref[:, :own] = total[: n_peer * own].astype(BF16).reshape(n_peer, own, LANES)
    for n in range(n_peer):
        out_ref[n, own:] = total[n_peer * own :].astype(BF16)


def end_kernel(got_ref, norm_ref, act_ref, grad_ref, weight_ref, out_act_ref):
    out_act_ref[...] = act_ref[...]
    total = got_ref[0].astype(F32)
    for n in range(1, got_ref.shape[0]):
        total = total + got_ref[n].astype(F32)
    part = grad_ref.shape[0]
    spot = 0
    for i in range(grad_ref.shape[1] // LANES):
        cut = slice(i * LANES, (i + 1) * LANES)
        grad_ref[:, cut] = (total[spot : spot + part] * norm_ref[:, cut]).astype(BF16)
        spot += part
    for j in range(weight_ref.shape[1] // LANES):
        weight_ref[:, j * LANES : (j + 1) * LANES] = total[spot : spot + part]
        spot += part


SMEM = pl.BlockSpec(memory_space=pltpu.SMEM)
VMEM = pl.BlockSpec(memory_space=pltpu.VMEM)
SCOPED = pltpu.CompilerParams(vmem_limit_bytes=24 * 2**20)


def call(kernel, outs, in_specs, *args, scratch=()):
    return pl.pallas_call(
        kernel,
        out_shape=outs,
        in_specs=in_specs,
        out_specs=jax.tree.map(lambda _: VMEM, outs),
        scratch_shapes=list(scratch),
        compiler_params=SCOPED,
    )(*args)


def per_device(features, weight, norm_scale, tile_rows, tile_cols, tile_vals, cotangent):
    rows_dev, part = features.shape
    tile_len = tile_vals.shape[1]
    row_tiles = rows_dev // tile_len
    hid_part = cotangent.shape[1]
    hidden = weight.shape[1]
    n_first = lax.axis_size(FIRST)
    n_second = lax.axis_size(SECOND)
    col_tiles = n_first * n_second * row_tiles
    norm = norm_scale.reshape(1, rows_dev)
    shape = jax.ShapeDtypeStruct

    block = (features.T.astype(F32) * norm_scale[None, :]).astype(BF16)
    for axes in OUT:
        block = jnp.broadcast_to(block[None], (lax.axis_size(axes),) + block.shape)
        block = lax.all_to_all(block, axes, 0, 0)
    group = call(
        forward_kernel,
        shape((lax.axis_size("zh"), 3 * part + hid_part, rows_dev), BF16),
        [SMEM, SMEM, VMEM, VMEM, VMEM, VMEM],
        tile_rows,
        tile_cols,
        tile_vals,
        block.reshape(n_first * n_second, part, rows_dev),
        weight,
        cotangent.T,
    )
    group = lax.all_gather(lax.all_to_all(group, "zh", 0, 0), "core", axis=0, tiled=True)
    own = row_tiles * part
    weight_rows = part * hidden // tile_len
    activated, sent = call(
        middle_kernel,
        (
            shape((hid_part, rows_dev), BF16),
            shape((n_first, n_second * own + weight_rows, tile_len), BF16),
        ),
        [SMEM, SMEM, VMEM, VMEM, VMEM, VMEM],
        tile_rows,
        tile_cols,
        tile_vals,
        group,
        weight,
        norm,
        scratch=(
            pltpu.VMEM((hidden, rows_dev), F32),
            pltpu.VMEM((col_tiles, part, tile_len), F32),
        ),
    )
    got = lax.all_to_all(sent, FIRST, 0, 0)
    sent = call(
        functools.partial(relay_kernel, own=own),
        shape((n_second, own + weight_rows, tile_len), BF16),
        [VMEM],
        got,
    )
    got = lax.all_to_all(sent, SECOND, 0, 0)
    feature_grad, weight_grad, activated = call(
        end_kernel,
        (
            shape((part, rows_dev), BF16),
            shape((part, hidden), F32),
            shape((hid_part, rows_dev), BF16),
        ),
        [VMEM, VMEM, VMEM],
        got,
        norm,
        activated,
    )
    return (activated.T, weight_grad, feature_grad.T)


OUT = (("y", "z"), "x")
FIRST, SECOND = ("x", "z"), "y"


def axes_of(rows, feats):
    return ((4, 8, 3) if rows == 96 else (2, rows // 4, 2)) + (feats // 2, 2)


def solution(mesh):
    sizes = axes_of(mesh.shape["row"], mesh.shape["feat"])
    fine = Mesh(mesh.devices.reshape(sizes), ("x", "y", "z", "zh", "core"))
    row, feat = ("x", "y", "z"), ("zh", "core")
    placed = (
        P(row, feat),
        P(feat, None),
        P(row),
        P(row),
        P(row),
        P(row, None, None),
        P(row, feat),
    )
    return jax.shard_map(
        per_device,
        mesh=fine,
        in_specs=placed,
        out_specs=(P(row, feat), P(feat, None), P(row, feat)),
        check_vma=False,
    )
```

```python
import functools

import jax
import jax.numpy as jnp
from jax import lax
from jax.experimental import pallas as pl
from jax.experimental.pallas import tpu as pltpu
from jax.sharding import Mesh, PartitionSpec as P

F32 = jnp.float32
BF16 = jnp.bfloat16
NT = (((1,), (1,)), ((), ()))
NN = (((1,), (0,)), ((), ()))
TN = (((0,), (0,)), ((), ()))
LANES = 128


def halves(value):
    head = value.astype(BF16)
    return head, (value - head.astype(F32)).astype(BF16)


def dot(left, right, dims):
    return lax.dot_general(left, right, dims, preferred_element_type=F32)


def spot_of(tile, row_tiles, orders):
    within, owner = lax.rem(tile, row_tiles), lax.div(tile, row_tiles)
    where = {}
    for axis in reversed(ROW):
        where[axis], owner = lax.rem(owner, lax.axis_size(axis)), lax.div(owner, lax.axis_size(axis))
    spot = 0
    for axis in [axis for order in orders for axis in order]:
        spot = spot * lax.axis_size(axis) + where[axis]
    return spot, within


def forward_kernel(rows_ref, cols_ref, tiles_ref, nodes_ref, weight_ref, cot_ref, out_ref):
    part = weight_ref.shape[0]
    row_tiles = cot_ref.shape[1] // LANES
    sums = jnp.zeros((row_tiles * part, LANES), F32)
    for t in range(0, tiles_ref.shape[0], 2):
        lefts = []
        for u in (t, t + 1):
            owner, within = spot_of(cols_ref[u], row_tiles, OUT[::-1])
            nodes = nodes_ref[owner, :, pl.ds(pl.multiple_of(within * LANES, LANES), LANES)]
            none = jnp.zeros_like(nodes)
            lefts.append(
                jnp.concatenate([jnp.where(rows_ref[u] == i, nodes, none) for i in range(row_tiles)], axis=0)
            )
        right = jnp.concatenate([tiles_ref[t], tiles_ref[t + 1]], axis=1)
        sums = sums + dot(jnp.concatenate(lefts, axis=1), right, NT)
    totals = [sums[i * part : (i + 1) * part] for i in range(row_tiles)]
    for i in range(row_tiles):
        head, rest = halves(totals[i])
        cut = slice(i * LANES, (i + 1) * LANES)
        for n in range(out_ref.shape[0]):
            out_ref[n, 0:part, cut] = head
            out_ref[n, part : 2 * part, cut] = rest
    for n in range(out_ref.shape[0]):
        out_ref[n, 2 * part : 3 * part] = weight_ref[...]
        out_ref[n, 3 * part :] = cot_ref[...]


def middle_kernel(
    rows_ref, cols_ref, tiles_ref, group_ref, weight_ref, norm_ref, act_ref, out_ref, pre_ref, total_ref
):
    my_zh, my_core = lax.axis_index("zh"), lax.axis_index("core")
    n_zh, n_core = lax.axis_size("zh"), lax.axis_size("core")
    me, my_place = my_zh * n_core + my_core, my_core * n_zh + my_zh
    part = weight_ref.shape[0]
    hid_part = act_ref.shape[0]
    n_feat = group_ref.shape[0]
    group = group_ref[...]
    head = group[:, 0:part].reshape(n_feat * part, -1)
    rest = group[:, part : 2 * part].reshape(n_feat * part, -1)
    weight_all = group[:, 2 * part : 3 * part].reshape(n_feat * part, -1)
    cot = jnp.concatenate(
        [group[core * n_zh + zh, 3 * part :] for zh in range(n_zh) for core in range(n_core)], axis=0
    )
    norm = norm_ref[...]
    pre = (dot(weight_all, head, TN) + dot(weight_all, rest, TN)) * norm
    pre_ref[...] = pre
    sigma = 1.0 / (1.0 + jnp.exp(-pre))
    slope = sigma * (1.0 + pre * (1.0 - sigma))
    back_in = (cot.astype(F32) * slope * norm).astype(BF16)
    own = pre_ref[pl.ds(pl.multiple_of(me * hid_part, hid_part), hid_part)]
    act_ref[...] = (own / (1.0 + jnp.exp(-own))).astype(BF16)

    back = dot(weight_ref[...], back_in, NN)
    row_tiles = back.shape[1] // LANES
    back_head, back_rest = halves(back)
    back_tiles = [
        jnp.concatenate([h[:, i * LANES : (i + 1) * LANES] for h in (back_head, back_rest)], axis=0)
        for i in range(row_tiles)
    ]
    total_ref[...] = jnp.zeros_like(total_ref)
    for t in range(tiles_ref.shape[0]):
        left = back_tiles[0]
        for i in range(1, row_tiles):
            left = jnp.where(rows_ref[t] == i, back_tiles[i], left)
        both = dot(left, tiles_ref[t], NN)
        owner, within = spot_of(cols_ref[t], row_tiles, BACK)
        total_ref[owner * row_tiles + within] += both[:part] + both[part:]

    own_head = group_ref[pl.ds(my_place, 1), 0:part][0]
    own_rest = group_ref[pl.ds(my_place, 1), part : 2 * part][0]
    weight_part = dot(own_head, back_in, NT) + dot(own_rest, back_in, NT)
    n_first, n_rows, _ = out_ref.shape
    cols = total_ref.shape[0] // n_first
    total = total_ref[...].astype(BF16).reshape(n_first, cols * part, LANES)
    out_ref[:, : cols * part] = total
    weight_part = weight_part.astype(BF16)
    spot = cols * part
    for j in range(weight_part.shape[1] // LANES):
        for n in range(n_first):
            out_ref[n, spot : spot + part] = weight_part[:, j * LANES : (j + 1) * LANES]
        spot += part


def relay_kernel(got_ref, out_ref, *, own):
    n_peer = out_ref.shape[0]
    total = got_ref[0].astype(F32)
    for n in range(1, got_ref.shape[0]):
        total = total + got_ref[n].astype(F32)
    out_ref[:, :own] = total[: n_peer * own].astype(BF16).reshape(n_peer, own, LANES)
    for n in range(n_peer):
        out_ref[n, own:] = total[n_peer * own :].astype(BF16)


def end_kernel(got_ref, norm_ref, act_ref, grad_ref, weight_ref, out_act_ref):
    out_act_ref[...] = act_ref[...]
    total = got_ref[0].astype(F32)
    for n in range(1, got_ref.shape[0]):
        total = total + got_ref[n].astype(F32)
    part = grad_ref.shape[0]
    spot = 0
    for i in range(grad_ref.shape[1] // LANES):
        cut = slice(i * LANES, (i + 1) * LANES)
        grad_ref[:, cut] = (total[spot : spot + part] * norm_ref[:, cut]).astype(BF16)
        spot += part
    for j in range(weight_ref.shape[1] // LANES):
        weight_ref[:, j * LANES : (j + 1) * LANES] = total[spot : spot + part]
        spot += part


SMEM = pl.BlockSpec(memory_space=pltpu.SMEM)
VMEM = pl.BlockSpec(memory_space=pltpu.VMEM)
SCOPED = pltpu.CompilerParams(vmem_limit_bytes=24 * 2**20)


def call(kernel, outs, in_specs, *args, scratch=()):
    return pl.pallas_call(
        kernel,
        out_shape=outs,
        in_specs=in_specs,
        out_specs=jax.tree.map(lambda _: VMEM, outs),
        scratch_shapes=list(scratch),
        compiler_params=SCOPED,
    )(*args)


def per_device(features, weight, norm_scale, tile_rows, tile_cols, tile_vals, cotangent):
    rows_dev, part = features.shape
    tile_len = tile_vals.shape[1]
    row_tiles = rows_dev // tile_len
    hid_part = cotangent.shape[1]
    hidden = weight.shape[1]
    n_first = lax.axis_size(BACK[0])
    n_second = lax.axis_size(BACK[1])
    col_tiles = n_first * n_second * row_tiles
    norm = norm_scale.reshape(1, rows_dev)
    shape = jax.ShapeDtypeStruct

    block = (features.T.astype(F32) * norm_scale[None, :]).astype(BF16)
    for axes in OUT:
        block = jnp.broadcast_to(block[None], (lax.axis_size(axes),) + block.shape)
        block = lax.all_to_all(block, axes, 0, 0)
    group = call(
        forward_kernel,
        shape((lax.axis_size("zh"), 3 * part + hid_part, rows_dev), BF16),
        [SMEM, SMEM, VMEM, VMEM, VMEM, VMEM],
        tile_rows,
        tile_cols,
        tile_vals,
        block.reshape(n_first * n_second, part, rows_dev),
        weight,
        cotangent.T,
    )
    group = lax.all_gather(lax.all_to_all(group, "zh", 0, 0), "core", axis=0, tiled=True)
    own = row_tiles * part
    weight_rows = part * hidden // tile_len
    activated, sent = call(
        middle_kernel,
        (
            shape((hid_part, rows_dev), BF16),
            shape((n_first, n_second * own + weight_rows, tile_len), BF16),
        ),
        [SMEM, SMEM, VMEM, VMEM, VMEM, VMEM],
        tile_rows,
        tile_cols,
        tile_vals,
        group,
        weight,
        norm,
        scratch=(
            pltpu.VMEM((hidden, rows_dev), F32),
            pltpu.VMEM((col_tiles, part, tile_len), F32),
        ),
    )
    got = lax.all_to_all(sent, BACK[0], 0, 0)
    sent = call(
        functools.partial(relay_kernel, own=own),
        shape((n_second, own + weight_rows, tile_len), BF16),
        [VMEM],
        got,
    )
    got = lax.all_to_all(sent, BACK[1], 0, 0)
    feature_grad, weight_grad, activated = call(
        end_kernel,
        (
            shape((part, rows_dev), BF16),
            shape((part, hidden), F32),
            shape((hid_part, rows_dev), BF16),
        ),
        [VMEM, VMEM, VMEM],
        got,
        norm,
        activated,
    )
    return (activated.T, weight_grad, feature_grad.T)


ROW, FEAT = ("x", "yh", "yl", "z"), ("zh", "core")
OUT = (("z", "yh"), ("yl", "x"))
BACK = (("yl", "x"), ("z", "yh"))


def axes_of(rows, feats):
    return ((4, 4, 2, 3) if rows == 96 else (2, rows // 4, 2, 1)) + (feats // 2, 2)


def solution(mesh):
    sizes = axes_of(mesh.shape["row"], mesh.shape["feat"])
    fine = Mesh(mesh.devices.reshape(sizes), ROW + FEAT)
    row, feat = ROW, FEAT
    placed = (
        P(row, feat),
        P(feat, None),
        P(row),
        P(row),
        P(row),
        P(row, None, None),
        P(row, feat),
    )
    return jax.shard_map(
        per_device,
        mesh=fine,
        in_specs=placed,
        out_specs=(P(row, feat), P(feat, None), P(row, feat)),
        check_vma=False,
    )
```

```python
import functools

import jax
import jax.numpy as jnp
import numpy as np
from jax import lax
from jax.experimental import pallas as pl
from jax.experimental.pallas import tpu as pltpu
from jax.sharding import Mesh, PartitionSpec as P

F32 = jnp.float32
BF16 = jnp.bfloat16
NT = (((1,), (1,)), ((), ()))
NN = (((1,), (0,)), ((), ()))
TN = (((0,), (0,)), ((), ()))
LANES = 128


def halves(value):
    head = value.astype(BF16)
    return head, (value - head.astype(F32)).astype(BF16)


def dot(left, right, dims):
    return lax.dot_general(left, right, dims, preferred_element_type=F32)


def spots(row_tiles):
    sizes = [lax.axis_size(axis) for axis in ROW]
    order = [ROW.index(axis) for axes in BACK for axis in axes]
    owners = np.arange(np.prod(sizes)).reshape(sizes).transpose(order).reshape(-1)
    table = np.empty((owners.size, row_tiles), np.int32)
    table[owners] = np.arange(owners.size * row_tiles).reshape(-1, row_tiles)
    return jnp.asarray(table.reshape(-1))


def forward_kernel(rows_ref, cols_ref, spots_ref, tiles_ref, nodes_ref, weight_ref, cot_ref, out_ref):
    part = weight_ref.shape[0]
    row_tiles = cot_ref.shape[1] // LANES
    sums = jnp.zeros((row_tiles * part, LANES), F32)
    for t in range(0, tiles_ref.shape[0], 2):
        lefts = []
        for u in (t, t + 1):
            spot = spots_ref[cols_ref[u]]
            owner, within = lax.div(spot, row_tiles), lax.rem(spot, row_tiles)
            nodes = nodes_ref[owner, :, pl.ds(pl.multiple_of(within * LANES, LANES), LANES)]
            none = jnp.zeros_like(nodes)
            lefts.append(
                jnp.concatenate([jnp.where(rows_ref[u] == i, nodes, none) for i in range(row_tiles)], axis=0)
            )
        right = jnp.concatenate([tiles_ref[t], tiles_ref[t + 1]], axis=1)
        sums = sums + dot(jnp.concatenate(lefts, axis=1), right, NT)
    totals = [sums[i * part : (i + 1) * part] for i in range(row_tiles)]
    for i in range(row_tiles):
        head, rest = halves(totals[i])
        cut = slice(i * LANES, (i + 1) * LANES)
        out_ref[0:part, cut] = head
        out_ref[part : 2 * part, cut] = rest
    out_ref[2 * part : 3 * part] = weight_ref[...]
    out_ref[3 * part :] = cot_ref[...]


def middle_kernel(
    rows_ref, cols_ref, spots_ref, tiles_ref, group_ref, weight_ref, norm_ref, act_ref, out_ref, pre_ref, total_ref
):
    me = lax.axis_index(FEAT)
    part = weight_ref.shape[0]
    hid_part = act_ref.shape[0]
    n_feat = group_ref.shape[0]
    group = group_ref[...]
    head = group[:, 0:part].reshape(n_feat * part, -1)
    rest = group[:, part : 2 * part].reshape(n_feat * part, -1)
    weight_all = group[:, 2 * part : 3 * part].reshape(n_feat * part, -1)
    cot = group[:, 3 * part :].reshape(n_feat * hid_part, -1)
    norm = norm_ref[...]
    pre = (dot(weight_all, head, TN) + dot(weight_all, rest, TN)) * norm
    pre_ref[...] = pre
    sigma = 1.0 / (1.0 + jnp.exp(-pre))
    slope = sigma * (1.0 + pre * (1.0 - sigma))
    back_in = (cot.astype(F32) * slope * norm).astype(BF16)
    own = pre_ref[pl.ds(pl.multiple_of(me * hid_part, hid_part), hid_part)]
    act_ref[...] = (own / (1.0 + jnp.exp(-own))).astype(BF16)

    back = dot(weight_ref[...], back_in, NN)
    row_tiles = back.shape[1] // LANES
    back_head, back_rest = halves(back)
    back_tiles = [
        jnp.concatenate([h[:, i * LANES : (i + 1) * LANES] for h in (back_head, back_rest)], axis=0)
        for i in range(row_tiles)
    ]
    total_ref[...] = jnp.zeros_like(total_ref)
    for t in range(tiles_ref.shape[0]):
        left = back_tiles[0]
        for i in range(1, row_tiles):
            left = jnp.where(rows_ref[t] == i, back_tiles[i], left)
        both = dot(left, tiles_ref[t], NN)
        total_ref[spots_ref[cols_ref[t]]] += both[:part] + both[part:]

    own_head = group_ref[pl.ds(me, 1), 0:part][0]
    own_rest = group_ref[pl.ds(me, 1), part : 2 * part][0]
    weight_part = dot(own_head, back_in, NT) + dot(own_rest, back_in, NT)
    n_first, n_rows, _ = out_ref.shape
    cols = total_ref.shape[0] // n_first
    total = total_ref[...].astype(BF16).reshape(n_first, cols * part, LANES)
    out_ref[:, : cols * part] = total
    weight_part = weight_part.astype(BF16)
    spot = cols * part
    for j in range(weight_part.shape[1] // LANES):
        for n in range(n_first):
            out_ref[n, spot : spot + part] = weight_part[:, j * LANES : (j + 1) * LANES]
        spot += part


def relay_kernel(got_ref, out_ref, *, own):
    n_peer = out_ref.shape[0]
    total = got_ref[0].astype(F32)
    for n in range(1, got_ref.shape[0]):
        total = total + got_ref[n].astype(F32)
    out_ref[:, :own] = total[: n_peer * own].astype(BF16).reshape(n_peer, own, LANES)
    for n in range(n_peer):
        out_ref[n, own:] = total[n_peer * own :].astype(BF16)


def end_kernel(got_ref, norm_ref, act_ref, grad_ref, weight_ref, out_act_ref):
    out_act_ref[...] = act_ref[...]
    total = got_ref[0].astype(F32)
    for n in range(1, got_ref.shape[0]):
        total = total + got_ref[n].astype(F32)
    part = grad_ref.shape[0]
    spot = 0
    for i in range(grad_ref.shape[1] // LANES):
        cut = slice(i * LANES, (i + 1) * LANES)
        grad_ref[:, cut] = (total[spot : spot + part] * norm_ref[:, cut]).astype(BF16)
        spot += part
    for j in range(weight_ref.shape[1] // LANES):
        weight_ref[:, j * LANES : (j + 1) * LANES] = total[spot : spot + part]
        spot += part


SMEM = pl.BlockSpec(memory_space=pltpu.SMEM)
VMEM = pl.BlockSpec(memory_space=pltpu.VMEM)
SCOPED = pltpu.CompilerParams(vmem_limit_bytes=24 * 2**20)


def call(kernel, outs, in_specs, *args, scratch=()):
    return pl.pallas_call(
        kernel,
        out_shape=outs,
        in_specs=in_specs,
        out_specs=jax.tree.map(lambda _: VMEM, outs),
        scratch_shapes=list(scratch),
        compiler_params=SCOPED,
    )(*args)


def per_device(features, weight, norm_scale, tile_rows, tile_cols, tile_vals, cotangent):
    rows_dev, part = features.shape
    tile_len = tile_vals.shape[1]
    row_tiles = rows_dev // tile_len
    hid_part = cotangent.shape[1]
    hidden = weight.shape[1]
    n_first = lax.axis_size(BACK[0])
    n_second = lax.axis_size(BACK[1])
    col_tiles = n_first * n_second * row_tiles
    norm = norm_scale.reshape(1, rows_dev)
    shape = jax.ShapeDtypeStruct
    table = spots(row_tiles)

    block = (features.T.astype(F32) * norm_scale[None, :]).astype(BF16)
    for axes in OUT:
        block = jnp.broadcast_to(block[None], (lax.axis_size(axes),) + block.shape)
        block = lax.all_to_all(block, axes, 0, 0)
    group = call(
        forward_kernel,
        shape((3 * part + hid_part, rows_dev), BF16),
        [SMEM, SMEM, SMEM, VMEM, VMEM, VMEM, VMEM],
        tile_rows,
        tile_cols,
        table,
        tile_vals,
        block.reshape(n_first * n_second, part, rows_dev),
        weight,
        cotangent.T,
    )
    group = lax.all_gather(group, FEAT)
    own = row_tiles * part
    weight_rows = part * hidden // tile_len
    activated, sent = call(
        middle_kernel,
        (
            shape((hid_part, rows_dev), BF16),
            shape((n_first, n_second * own + weight_rows, tile_len), BF16),
        ),
        [SMEM, SMEM, SMEM, VMEM, VMEM, VMEM, VMEM],
        tile_rows,
        tile_cols,
        table,
        tile_vals,
        group,
        weight,
        norm,
        scratch=(
            pltpu.VMEM((hidden, rows_dev), F32),
            pltpu.VMEM((col_tiles, part, tile_len), F32),
        ),
    )
    got = lax.all_to_all(sent, BACK[0], 0, 0)
    sent = call(
        functools.partial(relay_kernel, own=own),
        shape((n_second, own + weight_rows, tile_len), BF16),
        [VMEM],
        got,
    )
    got = lax.all_to_all(sent, BACK[1], 0, 0)
    feature_grad, weight_grad, activated = call(
        end_kernel,
        (
            shape((part, rows_dev), BF16),
            shape((part, hidden), F32),
            shape((hid_part, rows_dev), BF16),
        ),
        [VMEM, VMEM, VMEM],
        got,
        norm,
        activated,
    )
    return (activated.T, weight_grad, feature_grad.T)


ROW, FEAT = ("x", "yh", "yl", "z"), ("zh", "core")
OUT = (("z", "yh"), ("yl", "x"))
BACK = (("yl", "x"), ("z", "yh"))


def axes_of(rows, feats):
    return ((4, 4, 2, 3) if rows == 96 else (2, rows // 4, 2, 1)) + (feats // 2, 2)


def solution(mesh):
    sizes = axes_of(mesh.shape["row"], mesh.shape["feat"])
    fine = Mesh(mesh.devices.reshape(sizes), ROW + FEAT)
    row, feat = ROW, FEAT
    placed = (
        P(row, feat),
        P(feat, None),
        P(row),
        P(row),
        P(row),
        P(row, None, None),
        P(row, feat),
    )
    return jax.shard_map(
        per_device,
        mesh=fine,
        in_specs=placed,
        out_specs=(P(row, feat), P(feat, None), P(row, feat)),
        check_vma=False,
    )
```

```python
import functools

import jax
import jax.numpy as jnp
import numpy as np
from jax import lax
from jax.experimental import pallas as pl
from jax.experimental.pallas import tpu as pltpu
from jax.sharding import Mesh, PartitionSpec as P

F32 = jnp.float32
BF16 = jnp.bfloat16
NT = (((1,), (1,)), ((), ()))
NN = (((1,), (0,)), ((), ()))
TN = (((0,), (0,)), ((), ()))
LANES = 128


def halves(value):
    head = value.astype(BF16)
    return head, (value - head.astype(F32)).astype(BF16)


def dot(left, right, dims):
    return lax.dot_general(left, right, dims, preferred_element_type=F32)


def spots(row_tiles):
    sizes = [lax.axis_size(axis) for axis in ROW]
    order = [ROW.index(axis) for axes in BACK for axis in axes]
    owners = np.arange(np.prod(sizes)).reshape(sizes).transpose(order).reshape(-1)
    table = np.empty((owners.size, row_tiles), np.int32)
    table[owners] = np.arange(owners.size * row_tiles).reshape(-1, row_tiles)
    return jnp.asarray(table.reshape(-1))


def index_copies(sources, targets, sems):
    copies = [pltpu.make_async_copy(s, t, sems.at[i]) for i, (s, t) in enumerate(zip(sources, targets))]
    for copy in copies:
        copy.start()
    return copies


def forward_kernel(
    rows_in, cols_in, spots_in, tiles_ref, nodes_ref, weight_ref, cot_ref, out_ref, rows_ref, cols_ref, spots_ref, sems
):
    copies = index_copies((rows_in, cols_in, spots_in), (rows_ref, cols_ref, spots_ref), sems)
    part = weight_ref.shape[0]
    row_tiles = cot_ref.shape[1] // LANES
    out_ref[2 * part : 3 * part] = weight_ref[...]
    out_ref[3 * part :] = cot_ref[...]
    for copy in copies:
        copy.wait()
    sums = jnp.zeros((row_tiles * part, LANES), F32)
    for t in range(0, tiles_ref.shape[0], 2):
        lefts = []
        for u in (t, t + 1):
            spot = spots_ref[cols_ref[u]]
            owner, within = lax.div(spot, row_tiles), lax.rem(spot, row_tiles)
            nodes = nodes_ref[owner, :, pl.ds(pl.multiple_of(within * LANES, LANES), LANES)]
            none = jnp.zeros_like(nodes)
            lefts.append(
                jnp.concatenate([jnp.where(rows_ref[u] == i, nodes, none) for i in range(row_tiles)], axis=0)
            )
        right = jnp.concatenate([tiles_ref[t], tiles_ref[t + 1]], axis=1)
        sums = sums + dot(jnp.concatenate(lefts, axis=1), right, NT)
    totals = [sums[i * part : (i + 1) * part] for i in range(row_tiles)]
    for i in range(row_tiles):
        head, rest = halves(totals[i])
        cut = slice(i * LANES, (i + 1) * LANES)
        out_ref[0:part, cut] = head
        out_ref[part : 2 * part, cut] = rest


def middle_kernel(
    rows_in,
    cols_in,
    spots_in,
    tiles_ref,
    group_ref,
    weight_ref,
    norm_ref,
    act_ref,
    out_ref,
    pre_ref,
    total_ref,
    rows_ref,
    cols_ref,
    spots_ref,
    sems,
):
    copies = index_copies((rows_in, cols_in, spots_in), (rows_ref, cols_ref, spots_ref), sems)
    me = lax.axis_index(FEAT)
    part = weight_ref.shape[0]
    hid_part = act_ref.shape[0]
    n_feat = group_ref.shape[0]
    group = group_ref[...]
    head = group[:, 0:part].reshape(n_feat * part, -1)
    rest = group[:, part : 2 * part].reshape(n_feat * part, -1)
    weight_all = group[:, 2 * part : 3 * part].reshape(n_feat * part, -1)
    cot = group[:, 3 * part :].reshape(n_feat * hid_part, -1)
    norm = norm_ref[...]
    pre = dot(jnp.concatenate([weight_all] * 2, axis=0), jnp.concatenate([head, rest], axis=0), TN) * norm
    pre_ref[...] = pre
    sigma = 1.0 / (1.0 + jnp.exp(-pre))
    slope = sigma * (1.0 + pre * (1.0 - sigma))
    back_in = (cot.astype(F32) * slope * norm).astype(BF16)
    own = pre_ref[pl.ds(pl.multiple_of(me * hid_part, hid_part), hid_part)]
    act_ref[...] = (own / (1.0 + jnp.exp(-own))).astype(BF16)

    back = dot(weight_ref[...], back_in, NN)
    row_tiles = back.shape[1] // LANES
    back_head, back_rest = halves(back)
    left = jnp.concatenate(
        [h[:, i * LANES : (i + 1) * LANES] for i in range(row_tiles) for h in (back_head, back_rest)],
        axis=0,
    )
    total_ref[...] = jnp.zeros_like(total_ref)
    for copy in copies:
        copy.wait()
    for t in range(0, tiles_ref.shape[0], 2):
        wide = dot(left, jnp.concatenate([tiles_ref[t], tiles_ref[t + 1]], axis=1), NN)
        wide = wide.reshape(row_tiles, 2, part, -1)
        wide = [wide[i, 0] + wide[i, 1] for i in range(row_tiles)]
        for k in range(2):
            cut = slice(k * LANES, (k + 1) * LANES)
            term = wide[0][:, cut]
            for i in range(1, row_tiles):
                term = jnp.where(rows_ref[t + k] == i, wide[i][:, cut], term)
            total_ref[spots_ref[cols_ref[t + k]]] += term

    own = dot(group_ref[pl.ds(me, 1), 0 : 2 * part][0], back_in, NT)
    weight_part = own[:part] + own[part:]
    n_first, n_rows, _ = out_ref.shape
    cols = total_ref.shape[0] // n_first
    total = total_ref[...].astype(BF16).reshape(n_first, cols * part, LANES)
    out_ref[:, : cols * part] = total
    weight_part = weight_part.astype(BF16)
    spot = cols * part
    for j in range(weight_part.shape[1] // LANES):
        for n in range(n_first):
            out_ref[n, spot : spot + part] = weight_part[:, j * LANES : (j + 1) * LANES]
        spot += part


def relay_kernel(got_ref, out_ref, *, own):
    n_peer = out_ref.shape[0]
    total = got_ref[0].astype(F32)
    for n in range(1, got_ref.shape[0]):
        total = total + got_ref[n].astype(F32)
    out_ref[:, :own] = total[: n_peer * own].astype(BF16).reshape(n_peer, own, LANES)
    for n in range(n_peer):
        out_ref[n, own:] = total[n_peer * own :].astype(BF16)


def end_kernel(got_ref, norm_ref, act_ref, grad_ref, weight_ref, out_act_ref):
    out_act_ref[...] = act_ref[...]
    total = got_ref[0].astype(F32)
    for n in range(1, got_ref.shape[0]):
        total = total + got_ref[n].astype(F32)
    part = grad_ref.shape[0]
    spot = 0
    for i in range(grad_ref.shape[1] // LANES):
        cut = slice(i * LANES, (i + 1) * LANES)
        grad_ref[:, cut] = (total[spot : spot + part] * norm_ref[:, cut]).astype(BF16)
        spot += part
    for j in range(weight_ref.shape[1] // LANES):
        weight_ref[:, j * LANES : (j + 1) * LANES] = total[spot : spot + part]
        spot += part


VMEM = pl.BlockSpec(memory_space=pltpu.VMEM)
SCOPED = pltpu.CompilerParams(vmem_limit_bytes=24 * 2**20)


def call(kernel, outs, in_specs, *args, scratch=()):
    return pl.pallas_call(
        kernel,
        out_shape=outs,
        in_specs=in_specs,
        out_specs=jax.tree.map(lambda _: VMEM, outs),
        scratch_shapes=list(scratch),
        compiler_params=SCOPED,
    )(*args)


def per_device(features, weight, norm_scale, tile_rows, tile_cols, tile_vals, cotangent):
    rows_dev, part = features.shape
    tile_len = tile_vals.shape[1]
    row_tiles = rows_dev // tile_len
    hid_part = cotangent.shape[1]
    hidden = weight.shape[1]
    n_first = lax.axis_size(BACK[0])
    n_second = lax.axis_size(BACK[1])
    col_tiles = n_first * n_second * row_tiles
    norm = norm_scale.reshape(1, rows_dev)
    shape = jax.ShapeDtypeStruct
    table = spots(row_tiles)
    indices = tuple(pltpu.SMEM(a.shape, jnp.int32) for a in (tile_rows, tile_cols, table))
    indices += (pltpu.SemaphoreType.DMA((3,)),)

    block = (features.T.astype(F32) * norm_scale[None, :]).astype(BF16)
    for axes in OUT:
        block = jnp.broadcast_to(block[None], (lax.axis_size(axes),) + block.shape)
        block = lax.all_to_all(block, axes, 0, 0)
    group = call(
        forward_kernel,
        shape((3 * part + hid_part, rows_dev), BF16),
        [VMEM, VMEM, VMEM, VMEM, VMEM, VMEM, VMEM],
        tile_rows,
        tile_cols,
        table,
        tile_vals,
        block.reshape(n_first * n_second, part, rows_dev),
        weight,
        cotangent.T,
        scratch=indices,
    )
    group = lax.all_gather(group, FEAT)
    own = row_tiles * part
    weight_rows = part * hidden // tile_len
    activated, sent = call(
        middle_kernel,
        (
            shape((hid_part, rows_dev), BF16),
            shape((n_first, n_second * own + weight_rows, tile_len), BF16),
        ),
        [VMEM, VMEM, VMEM, VMEM, VMEM, VMEM, VMEM],
        tile_rows,
        tile_cols,
        table,
        tile_vals,
        group,
        weight,
        norm,
        scratch=(
            pltpu.VMEM((hidden, rows_dev), F32),
            pltpu.VMEM((col_tiles, part, tile_len), F32),
        )
        + indices,
    )
    got = lax.all_to_all(sent, BACK[0], 0, 0)
    sent = call(
        functools.partial(relay_kernel, own=own),
        shape((n_second, own + weight_rows, tile_len), BF16),
        [VMEM],
        got,
    )
    got = lax.all_to_all(sent, BACK[1], 0, 0)
    feature_grad, weight_grad, activated = call(
        end_kernel,
        (
            shape((part, rows_dev), BF16),
            shape((part, hidden), F32),
            shape((hid_part, rows_dev), BF16),
        ),
        [VMEM, VMEM, VMEM],
        got,
        norm,
        activated,
    )
    return (activated.T, weight_grad, feature_grad.T)


ROW, FEAT = ("x", "yh", "yl", "z"), ("zh", "core")
OUT = (("z", "yh"), ("yl", "x"))
BACK = (("yl", "x"), ("z", "yh"))


def axes_of(rows, feats):
    return ((4, 4, 2, 3) if rows == 96 else (2, rows // 4, 2, 1)) + (feats // 2, 2)


def solution(mesh):
    sizes = axes_of(mesh.shape["row"], mesh.shape["feat"])
    fine = Mesh(mesh.devices.reshape(sizes), ROW + FEAT)
    row, feat = ROW, FEAT
    placed = (
        P(row, feat),
        P(feat, None),
        P(row),
        P(row),
        P(row),
        P(row, None, None),
        P(row, feat),
    )
    return jax.shard_map(
        per_device,
        mesh=fine,
        in_specs=placed,
        out_specs=(P(row, feat), P(feat, None), P(row, feat)),
        check_vma=False,
    )
```

```python
import functools

import jax
import jax.numpy as jnp
import numpy as np
from jax import lax
from jax.experimental import pallas as pl
from jax.experimental.pallas import tpu as pltpu
from jax.sharding import Mesh, PartitionSpec as P

F32 = jnp.float32
BF16 = jnp.bfloat16
NT = (((1,), (1,)), ((), ()))
NN = (((1,), (0,)), ((), ()))
TN = (((0,), (0,)), ((), ()))
LANES = 128


def halves(value):
    head = value.astype(BF16)
    return head, (value - head.astype(F32)).astype(BF16)


def dot(left, right, dims):
    return lax.dot_general(left, right, dims, preferred_element_type=F32)


def spots(row_tiles):
    sizes = [lax.axis_size(axis) for axis in ROW]
    order = [ROW.index(axis) for axes in BACK for axis in axes]
    owners = np.arange(np.prod(sizes)).reshape(sizes).transpose(order).reshape(-1)
    table = np.empty((owners.size, row_tiles), np.int32)
    table[owners] = np.arange(owners.size * row_tiles).reshape(-1, row_tiles)
    return jnp.asarray(table.reshape(-1))


def index_copies(sources, targets, sems):
    copies = [pltpu.make_async_copy(s, t, sems.at[i]) for i, (s, t) in enumerate(zip(sources, targets))]
    for copy in copies:
        copy.start()
    return copies


def forward_kernel(
    rows_in, cols_in, spots_in, tiles_ref, nodes_ref, weight_ref, cot_ref, out_ref, own_ref, rows_ref, cols_ref, spots_ref, sems
):
    copies = index_copies((rows_in, cols_in, spots_in), (rows_ref, cols_ref, spots_ref), sems)
    part = weight_ref.shape[0]
    row_tiles = cot_ref.shape[1] // LANES
    out_ref[part : 2 * part] = weight_ref[...]
    out_ref[2 * part :] = cot_ref[...]
    for copy in copies:
        copy.wait()
    sums = jnp.zeros((row_tiles * part, LANES), F32)
    for t in range(0, tiles_ref.shape[0], 2):
        lefts = []
        for u in (t, t + 1):
            spot = spots_ref[cols_ref[u]]
            owner, within = lax.div(spot, row_tiles), lax.rem(spot, row_tiles)
            nodes = nodes_ref[owner, :, pl.ds(pl.multiple_of(within * LANES, LANES), LANES)]
            none = jnp.zeros_like(nodes)
            lefts.append(
                jnp.concatenate([jnp.where(rows_ref[u] == i, nodes, none) for i in range(row_tiles)], axis=0)
            )
        right = jnp.concatenate([tiles_ref[t], tiles_ref[t + 1]], axis=1)
        sums = sums + dot(jnp.concatenate(lefts, axis=1), right, NT)
    totals = [sums[i * part : (i + 1) * part] for i in range(row_tiles)]
    for i in range(row_tiles):
        head, rest = halves(totals[i])
        cut = slice(i * LANES, (i + 1) * LANES)
        out_ref[0:part, cut] = head
        own_ref[0:part, cut] = head
        own_ref[part:, cut] = rest


def middle_kernel(
    rows_in,
    cols_in,
    spots_in,
    tiles_ref,
    group_ref,
    own_ref,
    weight_ref,
    norm_ref,
    act_ref,
    out_ref,
    pre_ref,
    total_ref,
    rows_ref,
    cols_ref,
    spots_ref,
    sems,
):
    copies = index_copies((rows_in, cols_in, spots_in), (rows_ref, cols_ref, spots_ref), sems)
    me = lax.axis_index(FEAT)
    part = weight_ref.shape[0]
    hid_part = act_ref.shape[0]
    n_feat = group_ref.shape[0]
    group = group_ref[...]
    head = group[:, 0:part].reshape(n_feat * part, -1)
    weight_all = group[:, part : 2 * part].reshape(n_feat * part, -1)
    cot = group[:, 2 * part :].reshape(n_feat * hid_part, -1)
    norm = norm_ref[...]
    pre = dot(weight_all, head, TN) * norm
    pre_ref[...] = pre
    sigma = 1.0 / (1.0 + jnp.exp(-pre))
    slope = sigma * (1.0 + pre * (1.0 - sigma))
    back_in = (cot.astype(F32) * slope * norm).astype(BF16)
    own = pre_ref[pl.ds(pl.multiple_of(me * hid_part, hid_part), hid_part)]
    act_ref[...] = (own / (1.0 + jnp.exp(-own))).astype(BF16)

    back = dot(weight_ref[...], back_in, NN)
    row_tiles = back.shape[1] // LANES
    back_head, back_rest = halves(back)
    left = jnp.concatenate(
        [h[:, i * LANES : (i + 1) * LANES] for i in range(row_tiles) for h in (back_head, back_rest)],
        axis=0,
    )
    total_ref[...] = jnp.zeros_like(total_ref)
    for copy in copies:
        copy.wait()
    for t in range(0, tiles_ref.shape[0], 2):
        wide = dot(left, jnp.concatenate([tiles_ref[t], tiles_ref[t + 1]], axis=1), NN)
        wide = wide.reshape(row_tiles, 2, part, -1)
        wide = [wide[i, 0] + wide[i, 1] for i in range(row_tiles)]
        for k in range(2):
            cut = slice(k * LANES, (k + 1) * LANES)
            term = wide[0][:, cut]
            for i in range(1, row_tiles):
                term = jnp.where(rows_ref[t + k] == i, wide[i][:, cut], term)
            total_ref[spots_ref[cols_ref[t + k]]] += term

    own = dot(own_ref[...], back_in, NT)
    weight_part = own[:part] + own[part:]
    n_first, n_rows, _ = out_ref.shape
    cols = total_ref.shape[0] // n_first
    total = total_ref[...].astype(BF16).reshape(n_first, cols * part, LANES)
    out_ref[:, : cols * part] = total
    weight_part = weight_part.astype(BF16)
    spot = cols * part
    for j in range(weight_part.shape[1] // LANES):
        for n in range(n_first):
            out_ref[n, spot : spot + part] = weight_part[:, j * LANES : (j + 1) * LANES]
        spot += part


def relay_kernel(got_ref, out_ref, *, own):
    n_peer = out_ref.shape[0]
    total = got_ref[0].astype(F32)
    for n in range(1, got_ref.shape[0]):
        total = total + got_ref[n].astype(F32)
    out_ref[:, :own] = total[: n_peer * own].astype(BF16).reshape(n_peer, own, LANES)
    for n in range(n_peer):
        out_ref[n, own:] = total[n_peer * own :].astype(BF16)


def end_kernel(got_ref, norm_ref, act_ref, grad_ref, weight_ref, out_act_ref):
    out_act_ref[...] = act_ref[...]
    total = got_ref[0].astype(F32)
    for n in range(1, got_ref.shape[0]):
        total = total + got_ref[n].astype(F32)
    part = grad_ref.shape[0]
    spot = 0
    for i in range(grad_ref.shape[1] // LANES):
        cut = slice(i * LANES, (i + 1) * LANES)
        grad_ref[:, cut] = (total[spot : spot + part] * norm_ref[:, cut]).astype(BF16)
        spot += part
    for j in range(weight_ref.shape[1] // LANES):
        weight_ref[:, j * LANES : (j + 1) * LANES] = total[spot : spot + part]
        spot += part


VMEM = pl.BlockSpec(memory_space=pltpu.VMEM)
SCOPED = pltpu.CompilerParams(vmem_limit_bytes=24 * 2**20)


def call(kernel, outs, in_specs, *args, scratch=()):
    return pl.pallas_call(
        kernel,
        out_shape=outs,
        in_specs=in_specs,
        out_specs=jax.tree.map(lambda _: VMEM, outs),
        scratch_shapes=list(scratch),
        compiler_params=SCOPED,
    )(*args)


def per_device(features, weight, norm_scale, tile_rows, tile_cols, tile_vals, cotangent):
    rows_dev, part = features.shape
    tile_len = tile_vals.shape[1]
    row_tiles = rows_dev // tile_len
    hid_part = cotangent.shape[1]
    hidden = weight.shape[1]
    n_first = lax.axis_size(BACK[0])
    n_second = lax.axis_size(BACK[1])
    col_tiles = n_first * n_second * row_tiles
    norm = norm_scale.reshape(1, rows_dev)
    shape = jax.ShapeDtypeStruct
    table = spots(row_tiles)
    indices = tuple(pltpu.SMEM(a.shape, jnp.int32) for a in (tile_rows, tile_cols, table))
    indices += (pltpu.SemaphoreType.DMA((3,)),)

    block = (features.T.astype(F32) * norm_scale[None, :]).astype(BF16)
    for axes in OUT:
        block = jnp.broadcast_to(block[None], (lax.axis_size(axes),) + block.shape)
        block = lax.all_to_all(block, axes, 0, 0)
    group, own_mixed = call(
        forward_kernel,
        (shape((2 * part + hid_part, rows_dev), BF16), shape((2 * part, rows_dev), BF16)),
        [VMEM, VMEM, VMEM, VMEM, VMEM, VMEM, VMEM],
        tile_rows,
        tile_cols,
        table,
        tile_vals,
        block.reshape(n_first * n_second, part, rows_dev),
        weight,
        cotangent.T,
        scratch=indices,
    )
    group = lax.all_gather(group, FEAT)
    own = row_tiles * part
    weight_rows = part * hidden // tile_len
    activated, sent = call(
        middle_kernel,
        (
            shape((hid_part, rows_dev), BF16),
            shape((n_first, n_second * own + weight_rows, tile_len), BF16),
        ),
        [VMEM] * 8,
        tile_rows,
        tile_cols,
        table,
        tile_vals,
        group,
        own_mixed,
        weight,
        norm,
        scratch=(
            pltpu.VMEM((hidden, rows_dev), F32),
            pltpu.VMEM((col_tiles, part, tile_len), F32),
        )
        + indices,
    )
    got = lax.all_to_all(sent, BACK[0], 0, 0)
    sent = call(
        functools.partial(relay_kernel, own=own),
        shape((n_second, own + weight_rows, tile_len), BF16),
        [VMEM],
        got,
    )
    got = lax.all_to_all(sent, BACK[1], 0, 0)
    feature_grad, weight_grad, activated = call(
        end_kernel,
        (
            shape((part, rows_dev), BF16),
            shape((part, hidden), F32),
            shape((hid_part, rows_dev), BF16),
        ),
        [VMEM, VMEM, VMEM],
        got,
        norm,
        activated,
    )
    return (activated.T, weight_grad, feature_grad.T)


ROW, FEAT = ("x", "yh", "yl", "z"), ("zh", "core")
OUT = (("z", "yh"), ("yl", "x"))
BACK = (("yl", "x"), ("z", "yh"))


def axes_of(rows, feats):
    return ((4, 4, 2, 3) if rows == 96 else (2, rows // 4, 2, 1)) + (feats // 2, 2)


def solution(mesh):
    sizes = axes_of(mesh.shape["row"], mesh.shape["feat"])
    fine = Mesh(mesh.devices.reshape(sizes), ROW + FEAT)
    row, feat = ROW, FEAT
    placed = (
        P(row, feat),
        P(feat, None),
        P(row),
        P(row),
        P(row),
        P(row, None, None),
        P(row, feat),
    )
    return jax.shard_map(
        per_device,
        mesh=fine,
        in_specs=placed,
        out_specs=(P(row, feat), P(feat, None), P(row, feat)),
        check_vma=False,
    )
```
